32 devices in a mesh: groups: 2 (over y), expert: 4 (over x, core), replica: 4 (over z).
Axes of the slice: x: 2, y: 2, z: 4, core: 2. Of those that a mesh axis runs over, the one named last changes fastest.
Arguments:
- tokens: bfloat16 [768, 7168], P(('groups', 'expert'), 'replica'), parts along dimension 0, may hold values from -6 to 6
- expert_ids: int32 [768, 2], P(('groups', 'expert')), parts along dimension 0, may hold values from 0 to 3, all different within a row; in each aligned block of 96 rows (0 to 95, 96 to 191, ...) at most 60 rows name the same one
- affinity: float32 [768, 2], P(('groups', 'expert')), parts along dimension 0, may hold values from 0.05 to 1
- gate_up: bfloat16 [4, 7168, 2, 2048], P('expert', 'replica'), may hold values from -0.0625 to 0.0625
- down_proj: bfloat16 [4, 2048, 7168], P('expert', None, 'replica'), may hold values from -0.125 to 0.125
Outputs:
- mixed: bfloat16 [768, 7168], P(('groups', 'expert'), 'replica'), parts along dimension 0
The draws below stay inside these ranges and needn't reach their ends.
There are 2 independent parts, one for each index of `groups`. The reference program is written for one: setup_inputs(seed, part) draws one part's arguments, and reference() takes and returns one part's arrays. A program takes and returns all parts, laid end to end along the dimension named above; an argument that names none is the same for every part. Nothing has to cross between parts.
Inputs may be any that keep to these rules, and one draw needn't show every extreme that they name: `expert_ids`: each row names 2 different experts. Within each aligned block of 96 rows no expert is named by more than 60 rows, a bound that some block reaches.
All inputs are finite; a program needn't handle non-finite values.
Results may differ from the reference program's by a relative error of at most 0.023.
Values may be sent and summed in bfloat16 or wider, within the bound.
A program may use at most 128 MiB of HBM per device.

```python
import math
import jax
import jax.numpy as jnp
import numpy as np
from jax import lax

D = 7168
FF = 2048
TOK_DEV = 96
EXPERTS = 4
TOP = 2
CAP = 60
TOKENS = 384
N_EXPERT = 4
N_REPLICA = 4


def shard_levels(own_key, extent, shards, low, top_value):
    level, own = 1.0, jax.random.fold_in(own_key, 6)
    for dim, shards_of in shards:
        draws = jnp.exp(jax.random.uniform(jax.random.fold_in(own, dim), (shards_of,), jnp.float32, low / len(shards), top_value / len(shards)))
        level = level * jnp.repeat(draws, extent[dim] // shards_of).reshape([-1 if axis == dim else 1 for axis in range(len(extent))])
    return level


def deal_out(rng, own, number, rows, amount, top, limit, skew):
    order = jax.random.permutation(rng, amount)
    heavy_load, usual = shares(amount, rows * top, limit, skew, True), shares(amount, rows * top, limit, skew, False)
    places = jnp.arange(amount)

    def named(lengths, rotation):
        used = int((lengths > 0).sum())
        fixed = max(1, used // 4)
        shifted = fixed + (places - fixed + rotation * (used - fixed)) % max(1, amount - fixed)
        return jnp.zeros((amount,), jnp.int32).at[order[jnp.where(places < fixed, places, shifted)]].set(jnp.asarray(lengths, jnp.int32))

    lengths = jnp.where(number % 4 == 0, named(heavy_load, number // 4), named(usual, number - number // 4 - 1))
    mixed = jax.random.permutation(jax.random.fold_in(own, 3), amount)
    donor, sink = mixed[0:amount // 2 * 2:2], mixed[1:amount // 2 * 2:2]
    room = jnp.minimum(lengths[donor] - 1, limit - lengths[sink]) // 2
    room = jnp.where((donor == order[0]) | (sink == order[0]) | (lengths[sink] == 0), 0, jnp.maximum(room, 0))
    shifted = jax.random.randint(jax.random.fold_in(own, 4), (amount // 2,), 0, 1 << 20) % (room + 1)
    lengths = lengths.at[donor].add(-shifted).at[sink].add(shifted)
    members = jnp.searchsorted(jnp.cumsum(lengths), jnp.arange(rows * top), side="right").astype(jnp.int32)
    listing = members.reshape(top, rows).T
    listing = listing[jax.random.permutation(jax.random.fold_in(own, 1), rows)]
    rotation = jax.random.randint(jax.random.fold_in(own, 2), (rows, 1), 0, top)
    return jnp.take_along_axis(listing, (jnp.arange(top)[None, :] + rotation) % top, axis=1)


def shares(count, total, limit, slope, full):
    weights = [(1 << 20) // math.isqrt(grade ** slope) + 1 for grade in range(1, count + 1)]
    largest = limit if full else min(limit, max(-(-total // count), total * weights[0] // sum(weights)))
    least = 1 if total - largest >= count - 1 else 0
    counts, surplus = [largest] + [least] * (count - 1), total - largest - least * (count - 1)
    while surplus > 0:
        movable = [i for i in range(1, count) if counts[i] < largest] or [i for i in range(1, count) if counts[i] < limit]
        pool, left = sum([weights[i] for i in movable]), surplus
        for i in movable:
            extra = min(limit - counts[i], max(1, left * weights[i] // pool), surplus)
            counts[i] = counts[i] + extra
            surplus = surplus - extra
    return np.array(counts)


def noise(key, shape, spread, most, cuts=(), kind=jnp.bfloat16):
    entries = spread * jax.random.normal(key, shape, jnp.float32)
    if cuts:
        entries = entries * shard_levels(key, shape, cuts, -0.22, 0.18)
    return jnp.clip(entries, -most, most).astype(kind)


def setup_inputs(seed: int = 0, part: int = 0) -> dict:
    keys = jax.random.split(jax.random.key(seed), 6)
    part_splits = jax.random.split(jax.random.fold_in(keys[5], part), 6)
    tokens = noise(part_splits[0], (TOKENS, D), 1.0, 6.0, ((0, 4), (1, 4)))
    expert_ids_keys = jax.random.split(jax.random.fold_in(part_splits[1], 1), TOKENS // TOK_DEV)
    expert_ids_turns = jax.random.permutation(jax.random.fold_in(part_splits[1], 3), TOKENS // TOK_DEV)
    expert_ids = jax.vmap(lambda own, number: deal_out(jax.random.fold_in(part_splits[1], 2), own, number, TOK_DEV, EXPERTS, TOP, CAP, 2))(expert_ids_keys, expert_ids_turns).reshape((TOKENS, TOP))
    affinity = jnp.clip(0.05 + 0.95 * jax.random.uniform(part_splits[2], (TOKENS, TOP), jnp.float32) ** shard_levels(part_splits[2], (TOKENS, TOP), ((0, 4),), -0.2, 0.2), 0.05, 1.0)
    gate_up = noise(keys[3], (EXPERTS, D, 2, FF), D ** -0.5, 0.0625, ((0, 4), (1, 4)))
    down_proj = noise(keys[4], (EXPERTS, FF, D), FF ** -0.5, 0.125, ((0, 4), (2, 4)))
    return dict(tokens=tokens, expert_ids=expert_ids, affinity=affinity, gate_up=gate_up, down_proj=down_proj)


def reference(tokens, expert_ids, affinity, gate_up, down_proj):
    row_count = tokens.shape[0]
    slot_total = N_EXPERT * CAP
    width_slice = D // N_REPLICA
    weights = 2.5 * affinity / jnp.sum(affinity, axis=1, keepdims=True)
    token_index = jnp.arange(row_count, dtype=jnp.int32)
    padded = jnp.concatenate([tokens, jnp.zeros((1, D), tokens.dtype)], axis=0)

    def one_expert(running, expert_id):
        routed_mask = expert_ids == expert_id
        routed = jnp.any(routed_mask, axis=1)
        row_weight = jnp.sum(jnp.where(routed_mask, weights, jnp.zeros_like(weights)), axis=1)
        position = jnp.cumsum(routed.astype(jnp.int32)) - 1
        target = jnp.where(routed, position, slot_total).astype(jnp.int32)
        source = jnp.full((slot_total,), row_count, jnp.int32).at[target].set(token_index, mode="drop")
        chosen = padded[source]
        weight_pair = lax.dynamic_index_in_dim(gate_up, expert_id, 0, keepdims=False)
        sliced = chosen.astype(jnp.float32).reshape(slot_total, N_REPLICA, width_slice)
        weight_sliced = weight_pair.astype(jnp.float32).reshape(N_REPLICA, width_slice, 2 * FF)
        partials = jnp.einsum("rsd,sdf->srf", sliced, weight_sliced, precision=lax.Precision.HIGHEST)
        rounded = lax.optimization_barrier(partials.astype(jnp.bfloat16))
        pre_act = jnp.sum(rounded.astype(jnp.float32), axis=0).reshape(slot_total, 2, FF)
        hidden = (jax.nn.silu(pre_act[:, 0]) * pre_act[:, 1]).astype(jnp.bfloat16)
        down_rows = lax.dynamic_index_in_dim(down_proj, expert_id, 0, keepdims=False)
        expert_rows = jnp.dot(hidden, down_rows, preferred_element_type=jnp.float32).astype(jnp.bfloat16)
        slot_weight = jnp.concatenate([row_weight, jnp.zeros((1,), row_weight.dtype)])[source]
        running = running.at[source].add(slot_weight[:, None] * expert_rows.astype(slot_weight.dtype))
        return running, source

    initial = jnp.zeros((row_count + 1, D), jnp.float32)
    mixed, ignored = lax.scan(one_expert, initial, jnp.arange(EXPERTS, dtype=jnp.int32))
    return mixed[:row_count].astype(jnp.bfloat16)
```

```python
import functools

import jax
import jax.numpy as jnp
from jax import lax
from jax.experimental import pallas as pl
from jax.experimental.pallas import tpu as pltpu
from jax.sharding import PartitionSpec as P

MESH = pl.DeviceIdType.MESH
LANES = 128
SUBS = 2
LAG = 3


def slot_table(expert_ids, expert_count, stride):
    labels = lax.broadcasted_iota(jnp.int32, (1, 1, expert_count), 2)
    chosen = (expert_ids[:, :, None] == labels).astype(jnp.int32)
    per_row = jnp.sum(chosen, axis=1)
    before = jnp.cumsum(per_row, axis=0) - per_row
    slot_rank = jnp.sum(chosen * before[:, None, :], axis=2)
    return expert_ids * stride + slot_rank


def layer_kernel(
    n, depth, order, tokens, slots_t, slots, weights, gate_up, down, out,
    w_buf, d_buf, outgoing, x_buf, xs, acc, rs_in, rs_out, hid, res, ret,
    w_sem, d_sem, disp_s, disp_r, rs_s, rs_r, ag_s, ag_r, ret_s, ret_r,
):
    groups = lax.axis_index("groups")
    me = lax.axis_index("expert")
    z = lax.axis_index("replica")
    chip, core = me // 2, me % 2
    slot_rows = x_buf.shape[1]
    width = x_buf.shape[2]
    hidden = d_buf.shape[0]
    half = hidden // 2
    sub = half // SUBS
    blocks = sub // LANES
    units = n * SUBS
    sink = (0, depth - 1)
    source = (depth - 1, 0)
    onward = (z - 1, z + 1)
    back = (z + 1, z - 1)

    def w_copy(block):
        return pltpu.make_async_copy(
            gate_up.at[0, :, :, pl.ds(pl.multiple_of(block * LANES, LANES), LANES)],
            w_buf.at[block],
            w_sem.at[block],
        )

    for s in range(SUBS):
        for way in range(2):
            for i in range(blocks):
                w_copy((way * SUBS + s) * blocks + i).start()
    d_copy = pltpu.make_async_copy(down.at[0], d_buf, d_sem.at[0])
    d_copy.start()

    def partner(a, b, sign):
        return ((chip + sign * a + n // 2) % (n // 2)) * 2 + (core + b) % 2

    barrier = pltpu.get_barrier_semaphore()
    for a, b in order[1:]:
        pl.semaphore_signal(
            barrier, inc=1, device_id=(groups, partner(a, b, 1), z), device_id_type=MESH
        )

    @pl.when(z > 0)
    def _():
        pl.semaphore_signal(barrier, inc=1, device_id=(groups, me, z - 1), device_id_type=MESH)

    @pl.when(z < depth - 1)
    def _():
        pl.semaphore_signal(barrier, inc=1, device_id=(groups, me, z + 1), device_id_type=MESH)

    def pick(target):
        label = lax.broadcasted_iota(jnp.int32, (slot_rows, tokens.shape[0]), 0)
        label = label + target * slot_rows
        total = jnp.zeros(label.shape, jnp.float32)
        for k in range(slots_t.shape[0]):
            total = total + jnp.where(slots_t[k : k + 1, :] == label, 1.0, 0.0)
        return jnp.dot(
            total.astype(jnp.bfloat16), tokens[...], preferred_element_type=jnp.float32
        ).astype(jnp.bfloat16)

    x_buf[0] = pick(me)
    for k in range(1, n):
        a, b = order[k]
        outgoing[k - 1] = pick(partner(a, b, 1))

    at_end = jnp.logical_or(z == 0, z == depth - 1)

    @pl.when(at_end)
    def _():
        pl.semaphore_wait(barrier, n - 1 + min(1, depth - 1))

    @pl.when(jnp.logical_not(at_end))
    def _():
        pl.semaphore_wait(barrier, n + 1)

    def disp_copy(k, target):
        return pltpu.make_async_remote_copy(
            src_ref=outgoing.at[k - 1],
            dst_ref=x_buf.at[k],
            send_sem=disp_s.at[k],
            recv_sem=disp_r.at[k],
            device_id=(groups, target, z),
            device_id_type=MESH,
        )

    for k in range(1, n):
        a, b = order[k]
        disp_copy(k, partner(a, b, 1)).start()

    def rs_copy(u, way):
        return pltpu.make_async_remote_copy(
            src_ref=rs_out.at[u, way],
            dst_ref=rs_in.at[u, way],
            send_sem=rs_s.at[u, way],
            recv_sem=rs_r.at[u, way],
            device_id=(groups, me, onward[way]),
            device_id_type=MESH,
        )

    def ag_copy(u, way):
        return pltpu.make_async_remote_copy(
            src_ref=hid.at[u, way],
            dst_ref=hid.at[u, way],
            send_sem=ag_s.at[u, way],
            recv_sem=ag_r.at[u, way],
            device_id=(groups, me, back[way]),
            device_id_type=MESH,
        )

    def ret_copy(k, target):
        return pltpu.make_async_remote_copy(
            src_ref=res.at[k],
            dst_ref=ret.at[me],
            send_sem=ret_s.at[k],
            recv_sem=ret_r.at[k],
            device_id=(groups, target, z),
            device_id_type=MESH,
        )

    row = lax.broadcasted_iota(jnp.int32, (LANES, 2 * LANES), 0)
    column = lax.broadcasted_iota(jnp.int32, (LANES, 2 * LANES), 1)
    spread = [
        jnp.where(column == 2 * row + j, 1.0, 0.0).astype(jnp.bfloat16) for j in range(2)
    ]

    def reduce_step(u):
        k, s = u // SUBS, u % SUBS

        @pl.when(s == 0)
        def _():
            @pl.when(k > 0)
            def _():
                disp_copy(k, me).wait_recv()

            for block in range(width // LANES):
                part = x_buf[k, :, block * LANES : (block + 1) * LANES]
                for j in range(2):
                    xs[
                        j * slot_rows : (j + 1) * slot_rows,
                        2 * block * LANES : 2 * (block + 1) * LANES,
                    ] = jnp.dot(
                        part, spread[j], preferred_element_type=jnp.float32
                    ).astype(jnp.bfloat16)

        for way in range(2):
            first = (way * SUBS + s) * blocks

            @pl.when(u < SUBS)
            def _():
                for i in range(blocks):
                    w_copy(first + i).wait()

            for pair in range(blocks // 2):
                w = jnp.concatenate(
                    [
                        w_buf[first + 2 * pair + i].reshape(2 * width, LANES)
                        for i in range(2)
                    ],
                    axis=1,
                )
                acc[:, pair * 2 * LANES : (pair + 1) * 2 * LANES] = jnp.dot(
                    xs[...], w, preferred_element_type=jnp.float32
                )

            @pl.when(z != source[way])
            def _():
                rs_copy(u, way).wait_recv()
                acc[...] += rs_in[u, way].astype(jnp.float32)

            @pl.when(z != sink[way])
            def _():
                rs_out[u, way] = acc[...].astype(jnp.bfloat16)
                rs_copy(u, way).start()

            @pl.when(z == sink[way])
            def _():
                gate = acc[:slot_rows]
                hid[u, way] = (gate / (1.0 + jnp.exp(-gate)) * acc[slot_rows:]).astype(
                    jnp.bfloat16
                )
                ag_copy(u, way).start()

    def gather_step(v):
        k, s = v // SUBS, v % SUBS
        for way in range(2):

            @pl.when(z != sink[way])
            def _():
                ag_copy(v, way).wait_recv()

                @pl.when(z != source[way])
                def _():
                    ag_copy(v, way).start()

        @pl.when(s == SUBS - 1)
        def _():
            @pl.when(k == 0)
            def _():
                d_copy.wait()

            total = jnp.zeros((slot_rows, width), jnp.float32)
            for way in range(2):
                for i in range(SUBS):
                    start = way * half + i * sub
                    total = total + jnp.dot(
                        hid[k * SUBS + i, way],
                        d_buf[start : start + sub, :],
                        preferred_element_type=jnp.float32,
                    )

            @pl.when(k == 0)
            def _():
                ret[me] = total.astype(jnp.bfloat16)

            for kk in range(1, n):
                a, b = order[kk]

                @pl.when(k == kk)
                def _():
                    res[kk] = total.astype(jnp.bfloat16)
                    ret_copy(kk, partner(a, b, -1)).start()

    def step(u, carry):
        @pl.when(u < units)
        def _():
            reduce_step(u)

        @pl.when(u >= LAG)
        def _():
            gather_step(u - LAG)

        return carry

    lax.fori_loop(0, units + LAG, step, 0)

    def drain(u, carry):
        for way in range(2):

            @pl.when(z != sink[way])
            def _():
                rs_copy(u, way).wait_send()

            @pl.when(z != source[way])
            def _():
                ag_copy(u, way).wait_send()

        return carry

    lax.fori_loop(0, units, drain, 0)
    for k in range(1, n):
        disp_copy(k, me).wait_send()
        ret_copy(k, me).wait_send()
    for k in range(1, n):
        a, b = order[k]
        pltpu.make_async_remote_copy(
            src_ref=res.at[k],
            dst_ref=ret.at[partner(a, b, 1)],
            send_sem=ret_s.at[k],
            recv_sem=ret_r.at[k],
            device_id=(groups, me, z),
            device_id_type=MESH,
        ).wait_recv()

    rows = tokens.shape[0]
    label = lax.broadcasted_iota(jnp.int32, (rows, n * slot_rows), 1)
    chosen = [
        jnp.where(slots[:, k : k + 1] == label, 1.0, 0.0).astype(jnp.bfloat16)
        for k in range(slots.shape[1])
    ]
    tile = 2 * LANES if width % (2 * LANES) == 0 else LANES
    for c in range(width // tile):
        part = ret[:, :, c * tile : (c + 1) * tile].reshape(n * slot_rows, tile)
        mixed = jnp.zeros((rows, tile), jnp.float32)
        for k in range(slots.shape[1]):
            mixed = mixed + weights[:, k : k + 1] * jnp.dot(
                chosen[k], part, preferred_element_type=jnp.float32
            )
        out[:, c * tile : (c + 1) * tile] = mixed.astype(jnp.bfloat16)


def per_device(tokens, expert_ids, affinity, gate_up, down_proj):
    n = lax.axis_size("expert")
    depth = lax.axis_size("replica")
    rows, top = expert_ids.shape
    capacity = 5 * rows * top // (4 * n)
    slot_rows = -(-capacity // 16) * 16
    width = tokens.shape[1]
    hidden = down_proj.shape[1]
    slots = slot_table(expert_ids, n, slot_rows)
    weights = 2.5 * affinity / jnp.sum(affinity, axis=1, keepdims=True)
    order = [(0, 0)] + [(a, b) for a in range(1, n // 2) for b in range(2)] + [(0, 1)]
    units = n * SUBS
    sub = hidden // 2 // SUBS
    bf16 = jnp.bfloat16
    dma = pltpu.SemaphoreType.DMA
    vmem = pl.BlockSpec(memory_space=pltpu.VMEM)
    hbm = pl.BlockSpec(memory_space=pl.ANY)
    return pl.pallas_call(
        functools.partial(layer_kernel, n, depth, order),
        out_shape=jax.ShapeDtypeStruct((rows, width), bf16),
        in_specs=[vmem, vmem, vmem, vmem, hbm, hbm],
        out_specs=vmem,
        scratch_shapes=[
            pltpu.VMEM((hidden // LANES, width, 2, LANES), bf16),
            pltpu.VMEM((hidden, width), bf16),
            pltpu.VMEM((n - 1, slot_rows, width), bf16),
            pltpu.VMEM((n, slot_rows, width), bf16),
            pltpu.VMEM((2 * slot_rows, 2 * width), bf16),
            pltpu.VMEM((2 * slot_rows, sub), jnp.float32),
            pltpu.VMEM((units, 2, 2 * slot_rows, sub), bf16),
            pltpu.VMEM((units, 2, 2 * slot_rows, sub), bf16),
            pltpu.VMEM((units, 2, slot_rows, sub), bf16),
            pltpu.VMEM((n, slot_rows, width), bf16),
            pltpu.VMEM((n, slot_rows, width), bf16),
            dma((hidden // LANES,)),
            dma((1,)),
            dma((n,)),
            dma((n,)),
            dma((units, 2)),
            dma((units, 2)),
            dma((units, 2)),
            dma((units, 2)),
            dma((n,)),
            dma((n,)),
        ],
        compiler_params=pltpu.CompilerParams(
            collective_id=0, has_side_effects=True, vmem_limit_bytes=60 * 1024 * 1024
        ),
    )(tokens, slots.T, slots, weights, gate_up, down_proj)


def solution(mesh):
    placed = (
        P(("groups", "expert"), "replica"),
        P(("groups", "expert"), None),
        P(("groups", "expert"), None),
        P("expert", "replica", None, None),
        P("expert", None, "replica"),
    )
    return jax.shard_map(
        per_device,
        mesh=mesh,
        in_specs=placed,
        out_specs=P(("groups", "expert"), "replica"),
        check_vma=False,
    )
```

```python
import functools

import jax
import jax.numpy as jnp
from jax import lax
from jax.experimental import pallas as pl
from jax.experimental.pallas import tpu as pltpu
from jax.sharding import PartitionSpec as P

MESH = pl.DeviceIdType.MESH
LANES = 128
SUBS = 2
PIECES = 4
LAG = 3


def slot_table(expert_ids, expert_count, stride):
    labels = lax.broadcasted_iota(jnp.int32, (1, 1, expert_count), 2)
    chosen = (expert_ids[:, :, None] == labels).astype(jnp.int32)
    per_row = jnp.sum(chosen, axis=1)
    before = jnp.cumsum(per_row, axis=0) - per_row
    slot_rank = jnp.sum(chosen * before[:, None, :], axis=2)
    return expert_ids * stride + slot_rank


def layer_kernel(
    n, depth, order, tokens, slots_t, slots, weights, gate_up, down, out,
    w_buf, d_buf, outgoing, x_buf, xs, acc, rs_in, rs_out, hid, res, ret,
    w_sem, d_sem, disp_s, disp_r, rs_s, rs_r, ag_s, ag_r, ret_s, ret_r,
):
    groups = lax.axis_index("groups")
    me = lax.axis_index("expert")
    z = lax.axis_index("replica")
    chip, core = me // 2, me % 2
    slot_rows = x_buf.shape[1]
    width = x_buf.shape[2]
    hidden = d_buf.shape[0]
    half = hidden // 2
    sub = half // SUBS
    units = n * SUBS
    sink = (0, depth - 1)
    source = (depth - 1, 0)
    onward = (z - 1, z + 1)
    back = (z + 1, z - 1)

    cut = 2 * width // PIECES

    def w_copy(block, piece):
        return pltpu.make_async_copy(
            gate_up.at[0]
            .reshape(2 * width, hidden)
            .at[pl.ds(piece * cut, cut), pl.ds(pl.multiple_of(block * sub, sub), sub)],
            w_buf.at[block, pl.ds(piece * cut, cut)],
            w_sem.at[block, piece],
        )

    for s in range(SUBS):
        for way in range(2):
            for piece in range(PIECES):
                w_copy(way * SUBS + s, piece).start()
    d_copy = pltpu.make_async_copy(down.at[0], d_buf, d_sem.at[0])
    d_copy.start()

    def partner(a, b, sign):
        return ((chip + sign * a + n // 2) % (n // 2)) * 2 + (core + b) % 2

    barrier = pltpu.get_barrier_semaphore()
    for a, b in order[1:]:
        pl.semaphore_signal(
            barrier, inc=1, device_id=(groups, partner(a, b, 1), z), device_id_type=MESH
        )

    @pl.when(z > 0)
    def _():
        pl.semaphore_signal(barrier, inc=1, device_id=(groups, me, z - 1), device_id_type=MESH)

    @pl.when(z < depth - 1)
    def _():
        pl.semaphore_signal(barrier, inc=1, device_id=(groups, me, z + 1), device_id_type=MESH)

    def pick(target):
        label = lax.broadcasted_iota(jnp.int32, (slot_rows, tokens.shape[0]), 0)
        label = label + target * slot_rows
        total = jnp.zeros(label.shape, jnp.float32)
        for k in range(slots_t.shape[0]):
            total = total + jnp.where(slots_t[k : k + 1, :] == label, 1.0, 0.0)
        return jnp.dot(
            total.astype(jnp.bfloat16), tokens[...], preferred_element_type=jnp.float32
        ).astype(jnp.bfloat16)

    x_buf[0] = pick(me)
    for k in range(1, n):
        a, b = order[k]
        outgoing[k - 1] = pick(partner(a, b, 1))

    at_end = jnp.logical_or(z == 0, z == depth - 1)

    @pl.when(at_end)
    def _():
        pl.semaphore_wait(barrier, n - 1 + min(1, depth - 1))

    @pl.when(jnp.logical_not(at_end))
    def _():
        pl.semaphore_wait(barrier, n + 1)

    def disp_copy(k, target):
        return pltpu.make_async_remote_copy(
            src_ref=outgoing.at[k - 1],
            dst_ref=x_buf.at[k],
            send_sem=disp_s.at[k],
            recv_sem=disp_r.at[k],
            device_id=(groups, target, z),
            device_id_type=MESH,
        )

    for k in range(1, n):
        a, b = order[k]
        disp_copy(k, partner(a, b, 1)).start()

    def rs_copy(u, way):
        return pltpu.make_async_remote_copy(
            src_ref=rs_out.at[u, way],
            dst_ref=rs_in.at[u, way],
            send_sem=rs_s.at[u, way],
            recv_sem=rs_r.at[u, way],
            device_id=(groups, me, onward[way]),
            device_id_type=MESH,
        )

    def ag_copy(u, way):
        return pltpu.make_async_remote_copy(
            src_ref=hid.at[u, way],
            dst_ref=hid.at[u, way],
            send_sem=ag_s.at[u, way],
            recv_sem=ag_r.at[u, way],
            device_id=(groups, me, back[way]),
            device_id_type=MESH,
        )

    def ret_copy(k, target):
        return pltpu.make_async_remote_copy(
            src_ref=res.at[k],
            dst_ref=ret.at[me],
            send_sem=ret_s.at[k],
            recv_sem=ret_r.at[k],
            device_id=(groups, target, z),
            device_id_type=MESH,
        )

    row = lax.broadcasted_iota(jnp.int32, (LANES, 2 * LANES), 0)
    column = lax.broadcasted_iota(jnp.int32, (LANES, 2 * LANES), 1)
    spread = [
        jnp.where(column == 2 * row + j, 1.0, 0.0).astype(jnp.bfloat16) for j in range(2)
    ]

    def reduce_step(u):
        k, s = u // SUBS, u % SUBS

        @pl.when(s == 0)
        def _():
            @pl.when(k > 0)
            def _():
                disp_copy(k, me).wait_recv()

            for block in range(width // LANES):
                part = x_buf[k, :, block * LANES : (block + 1) * LANES]
                for j in range(2):
                    xs[
                        j * slot_rows : (j + 1) * slot_rows,
                        2 * block * LANES : 2 * (block + 1) * LANES,
                    ] = jnp.dot(
                        part, spread[j], preferred_element_type=jnp.float32
                    ).astype(jnp.bfloat16)

        for way in range(2):
            block = way * SUBS + s

            @pl.when(u < SUBS)
            def _():
                for piece in range(PIECES):
                    w_copy(block, piece).wait()

            acc[...] = jnp.dot(xs[...], w_buf[block], preferred_element_type=jnp.float32)

            @pl.when(z != source[way])
            def _():
                rs_copy(u, way).wait_recv()
                acc[...] += rs_in[u, way].astype(jnp.float32)

            @pl.when(z != sink[way])
            def _():
                rs_out[u, way] = acc[...].astype(jnp.bfloat16)
                rs_copy(u, way).start()

            @pl.when(z == sink[way])
            def _():
                gate = acc[:slot_rows]
                hid[u, way] = (gate / (1.0 + jnp.exp(-gate)) * acc[slot_rows:]).astype(
                    jnp.bfloat16
                )
                ag_copy(u, way).start()

    def gather_step(v):
        k, s = v // SUBS, v % SUBS
        for way in range(2):

            @pl.when(z != sink[way])
            def _():
                ag_copy(v, way).wait_recv()

                @pl.when(z != source[way])
                def _():
                    ag_copy(v, way).start()

        @pl.when(s == SUBS - 1)
        def _():
            @pl.when(k == 0)
            def _():
                d_copy.wait()

            total = jnp.zeros((slot_rows, width), jnp.float32)
            for way in range(2):
                for i in range(SUBS):
                    start = way * half + i * sub
                    total = total + jnp.dot(
                        hid[k * SUBS + i, way],
                        d_buf[start : start + sub, :],
                        preferred_element_type=jnp.float32,
                    )

            @pl.when(k == 0)
            def _():
                ret[me] = total.astype(jnp.bfloat16)

            for kk in range(1, n):
                a, b = order[kk]

                @pl.when(k == kk)
                def _():
                    res[kk] = total.astype(jnp.bfloat16)
                    ret_copy(kk, partner(a, b, -1)).start()

    def step(u, carry):
        @pl.when(u < units)
        def _():
            reduce_step(u)

        @pl.when(u >= LAG)
        def _():
            gather_step(u - LAG)

        return carry

    lax.fori_loop(0, units + LAG, step, 0)

    def drain(u, carry):
        for way in range(2):

            @pl.when(z != sink[way])
            def _():
                rs_copy(u, way).wait_send()

            @pl.when(z != source[way])
            def _():
                ag_copy(u, way).wait_send()

        return carry

    lax.fori_loop(0, units, drain, 0)
    for k in range(1, n):
        disp_copy(k, me).wait_send()
        ret_copy(k, me).wait_send()
    for k in range(1, n):
        a, b = order[k]
        pltpu.make_async_remote_copy(
            src_ref=res.at[k],
            dst_ref=ret.at[partner(a, b, 1)],
            send_sem=ret_s.at[k],
            recv_sem=ret_r.at[k],
            device_id=(groups, me, z),
            device_id_type=MESH,
        ).wait_recv()

    rows = tokens.shape[0]
    label = lax.broadcasted_iota(jnp.int32, (rows, n * slot_rows), 1)
    chosen = [
        jnp.where(slots[:, k : k + 1] == label, 1.0, 0.0).astype(jnp.bfloat16)
        for k in range(slots.shape[1])
    ]
    tile = 2 * LANES if width % (2 * LANES) == 0 else LANES
    for c in range(width // tile):
        part = ret[:, :, c * tile : (c + 1) * tile].reshape(n * slot_rows, tile)
        mixed = jnp.zeros((rows, tile), jnp.float32)
        for k in range(slots.shape[1]):
            mixed = mixed + weights[:, k : k + 1] * jnp.dot(
                chosen[k], part, preferred_element_type=jnp.float32
            )
        out[:, c * tile : (c + 1) * tile] = mixed.astype(jnp.bfloat16)


def per_device(tokens, expert_ids, affinity, gate_up, down_proj):
    n = lax.axis_size("expert")
    depth = lax.axis_size("replica")
    rows, top = expert_ids.shape
    capacity = 5 * rows * top // (4 * n)
    slot_rows = -(-capacity // 16) * 16
    width = tokens.shape[1]
    hidden = down_proj.shape[1]
    slots = slot_table(expert_ids, n, slot_rows)
    weights = 2.5 * affinity / jnp.sum(affinity, axis=1, keepdims=True)
    order = [(0, 0)] + [(a, b) for a in range(1, n // 2) for b in range(2)] + [(0, 1)]
    units = n * SUBS
    sub = hidden // 2 // SUBS
    bf16 = jnp.bfloat16
    dma = pltpu.SemaphoreType.DMA
    vmem = pl.BlockSpec(memory_space=pltpu.VMEM)
    hbm = pl.BlockSpec(memory_space=pl.ANY)
    return pl.pallas_call(
        functools.partial(layer_kernel, n, depth, order),
        out_shape=jax.ShapeDtypeStruct((rows, width), bf16),
        in_specs=[vmem, vmem, vmem, vmem, hbm, hbm],
        out_specs=vmem,
        scratch_shapes=[
            pltpu.VMEM((2 * SUBS, 2 * width, sub), bf16),
            pltpu.VMEM((hidden, width), bf16),
            pltpu.VMEM((n - 1, slot_rows, width), bf16),
            pltpu.VMEM((n, slot_rows, width), bf16),
            pltpu.VMEM((2 * slot_rows, 2 * width), bf16),
            pltpu.VMEM((2 * slot_rows, sub), jnp.float32),
            pltpu.VMEM((units, 2, 2 * slot_rows, sub), bf16),
            pltpu.VMEM((units, 2, 2 * slot_rows, sub), bf16),
            pltpu.VMEM((units, 2, slot_rows, sub), bf16),
            pltpu.VMEM((n, slot_rows, width), bf16),
            pltpu.VMEM((n, slot_rows, width), bf16),
            dma((2 * SUBS, PIECES)),
            dma((1,)),
            dma((n,)),
            dma((n,)),
            dma((units, 2)),
            dma((units, 2)),
            dma((units, 2)),
            dma((units, 2)),
            dma((n,)),
            dma((n,)),
        ],
        compiler_params=pltpu.CompilerParams(
            collective_id=0, has_side_effects=True, vmem_limit_bytes=60 * 1024 * 1024
        ),
    )(tokens, slots.T, slots, weights, gate_up, down_proj)


def solution(mesh):
    placed = (
        P(("groups", "expert"), "replica"),
        P(("groups", "expert"), None),
        P(("groups", "expert"), None),
        P("expert", "replica", None, None),
        P("expert", None, "replica"),
    )
    return jax.shard_map(
        per_device,
        mesh=mesh,
        in_specs=placed,
        out_specs=P(("groups", "expert"), "replica"),
        check_vma=False,
    )
```

```python
import functools

import jax
import jax.numpy as jnp
from jax import lax
from jax.experimental import pallas as pl
from jax.experimental.pallas import tpu as pltpu
from jax.sharding import PartitionSpec as P

MESH = pl.DeviceIdType.MESH
LANES = 128
SUBS = 4
PIECES = 2
SKEW = 2


def slot_table(expert_ids, expert_count, stride):
    labels = lax.broadcasted_iota(jnp.int32, (1, 1, expert_count), 2)
    chosen = (expert_ids[:, :, None] == labels).astype(jnp.int32)
    per_row = jnp.sum(chosen, axis=1)
    before = jnp.cumsum(per_row, axis=0) - per_row
    slot_rank = jnp.sum(chosen * before[:, None, :], axis=2)
    return expert_ids * stride + slot_rank


def layer_kernel(
    n, depth, order, tokens, slots_t, slots, weights, gate_up, down, out,
    w_buf, d_buf, outgoing, x_buf, xs, acc, rs_in, rs_out, hid, res, ret,
    w_sem, d_sem, disp_s, disp_r, rs_s, rs_r, ag_s, ag_r, ret_s, ret_r,
):
    groups = lax.axis_index("groups")
    me = lax.axis_index("expert")
    z = lax.axis_index("replica")
    chip, core = me // 2, me % 2
    slot_rows = x_buf.shape[1]
    width = x_buf.shape[2]
    hidden = d_buf.shape[0]
    half = hidden // 2
    sub = half // SUBS
    units = n * SUBS
    sink = (0, depth - 1)
    source = (depth - 1, 0)
    onward = (z - 1, z + 1)
    back = (z + 1, z - 1)

    cut = 2 * width // PIECES

    def w_copy(block, piece):
        return pltpu.make_async_copy(
            gate_up.at[0]
            .reshape(2 * width, hidden)
            .at[pl.ds(piece * cut, cut), pl.ds(pl.multiple_of(block * sub, sub), sub)],
            w_buf.at[block, pl.ds(piece * cut, cut)],
            w_sem.at[block, piece],
        )

    for s in range(SUBS):
        for way in range(2):
            for piece in range(PIECES):
                w_copy(way * SUBS + s, piece).start()
    d_copy = pltpu.make_async_copy(down.at[0], d_buf, d_sem.at[0])
    d_copy.start()

    def partner(a, b, sign):
        return ((chip + sign * a + n // 2) % (n // 2)) * 2 + (core + b) % 2

    barrier = pltpu.get_barrier_semaphore()
    for a, b in order[1:]:
        pl.semaphore_signal(
            barrier, inc=1, device_id=(groups, partner(a, b, 1), z), device_id_type=MESH
        )

    @pl.when(z > 0)
    def _():
        pl.semaphore_signal(barrier, inc=1, device_id=(groups, me, z - 1), device_id_type=MESH)

    @pl.when(z < depth - 1)
    def _():
        pl.semaphore_signal(barrier, inc=1, device_id=(groups, me, z + 1), device_id_type=MESH)

    def pick(target):
        label = lax.broadcasted_iota(jnp.int32, (slot_rows, tokens.shape[0]), 0)
        label = label + target * slot_rows
        total = jnp.zeros(label.shape, jnp.float32)
        for k in range(slots_t.shape[0]):
            total = total + jnp.where(slots_t[k : k + 1, :] == label, 1.0, 0.0)
        return jnp.dot(
            total.astype(jnp.bfloat16), tokens[...], preferred_element_type=jnp.float32
        ).astype(jnp.bfloat16)

    x_buf[0] = pick(me)
    for k in range(1, n):
        a, b = order[k]
        outgoing[k - 1] = pick(partner(a, b, 1))

    at_end = jnp.logical_or(z == 0, z == depth - 1)

    @pl.when(at_end)
    def _():
        pl.semaphore_wait(barrier, n - 1 + min(1, depth - 1))

    @pl.when(jnp.logical_not(at_end))
    def _():
        pl.semaphore_wait(barrier, n + 1)

    def disp_copy(k, target):
        return pltpu.make_async_remote_copy(
            src_ref=outgoing.at[k - 1],
            dst_ref=x_buf.at[k],
            send_sem=disp_s.at[k],
            recv_sem=disp_r.at[k],
            device_id=(groups, target, z),
            device_id_type=MESH,
        )

    for k in range(1, n):
        a, b = order[k]
        disp_copy(k, partner(a, b, 1)).start()

    def rs_copy(u, way):
        return pltpu.make_async_remote_copy(
            src_ref=rs_out.at[u, way],
            dst_ref=rs_in.at[u, way],
            send_sem=rs_s.at[u, way],
            recv_sem=rs_r.at[u, way],
            device_id=(groups, me, onward[way]),
            device_id_type=MESH,
        )

    def ag_copy(u, way):
        return pltpu.make_async_remote_copy(
            src_ref=hid.at[u, way],
            dst_ref=hid.at[u, way],
            send_sem=ag_s.at[u, way],
            recv_sem=ag_r.at[u, way],
            device_id=(groups, me, back[way]),
            device_id_type=MESH,
        )

    def ret_copy(k, target):
        return pltpu.make_async_remote_copy(
            src_ref=res.at[k],
            dst_ref=ret.at[me],
            send_sem=ret_s.at[k],
            recv_sem=ret_r.at[k],
            device_id=(groups, target, z),
            device_id_type=MESH,
        )

    row = lax.broadcasted_iota(jnp.int32, (LANES, 2 * LANES), 0)
    column = lax.broadcasted_iota(jnp.int32, (LANES, 2 * LANES), 1)
    spread = [
        jnp.where(column == 2 * row + j, 1.0, 0.0).astype(jnp.bfloat16) for j in range(2)
    ]

    position = (depth - 1 - z, z)
    nearest = jnp.minimum(position[0], position[1])
    furthest = jnp.maximum(position[0], position[1])
    fill = SKEW * (depth - 1)

    def live(u):
        return jnp.logical_and(u >= 0, u < units)

    def widen(k):
        @pl.when(k > 0)
        def _():
            disp_copy(k, me).wait_recv()

        for block in range(width // LANES):
            part = x_buf[k, :, block * LANES : (block + 1) * LANES]
            for j in range(2):
                xs[
                    k,
                    j * slot_rows : (j + 1) * slot_rows,
                    2 * block * LANES : 2 * (block + 1) * LANES,
                ] = jnp.dot(part, spread[j], preferred_element_type=jnp.float32).astype(
                    jnp.bfloat16
                )

    def multiply(u, way):
        block = way * SUBS + u % SUBS

        @pl.when(u < SUBS)
        def _():
            for piece in range(PIECES):
                w_copy(block, piece).wait()

        acc[way] = jnp.dot(
            xs[u // SUBS], w_buf[block], preferred_element_type=jnp.float32
        )

    def reduce_step(u, way):
        @pl.when(z != source[way])
        def _():
            rs_copy(u, way).wait_recv()
            acc[way] += rs_in[u, way].astype(jnp.float32)

        @pl.when(z != sink[way])
        def _():
            rs_out[u, way] = acc[way].astype(jnp.bfloat16)
            rs_copy(u, way).start()

        @pl.when(z == sink[way])
        def _():
            gate = acc[way, :slot_rows]
            hid[u, way] = (gate / (1.0 + jnp.exp(-gate)) * acc[way, slot_rows:]).astype(
                jnp.bfloat16
            )
            ag_copy(u, way).start()

    def gather_step(v, way):
        @pl.when(z != sink[way])
        def _():
            ag_copy(v, way).wait_recv()

            @pl.when(z != source[way])
            def _():
                ag_copy(v, way).start()

    def project(k):
        @pl.when(k == 0)
        def _():
            d_copy.wait()

        total = jnp.zeros((slot_rows, width), jnp.float32)
        for way in range(2):
            for i in range(SUBS):
                start = way * half + i * sub
                total = total + jnp.dot(
                    hid[k * SUBS + i, way],
                    d_buf[start : start + sub, :],
                    preferred_element_type=jnp.float32,
                )

        @pl.when(k == 0)
        def _():
            ret[me] = total.astype(jnp.bfloat16)

        for kk in range(1, n):
            a, b = order[kk]

            @pl.when(k == kk)
            def _():
                res[kk] = total.astype(jnp.bfloat16)
                ret_copy(kk, partner(a, b, -1)).start()

    def step(t, carry):
        lead = t - SKEW * nearest

        @pl.when(jnp.logical_and(live(lead), lead % SUBS == 0))
        def _():
            widen(lead // SUBS)

        for way in range(2):
            u = t - SKEW * position[way]

            @pl.when(live(u))
            def _():
                multiply(u, way)

        for way in range(2):
            u = t - SKEW * position[way]

            @pl.when(live(u))
            def _():
                reduce_step(u, way)

        for way in range(2):
            v = t - fill - SKEW * (depth - 1 - position[way])

            @pl.when(live(v))
            def _():
                gather_step(v, way)

        trail = t - fill - SKEW * furthest

        @pl.when(jnp.logical_and(live(trail), trail % SUBS == SUBS - 1))
        def _():
            project(trail // SUBS)

        return carry

    lax.fori_loop(0, units + 2 * fill, step, 0)

    def drain(u, carry):
        for way in range(2):

            @pl.when(z != sink[way])
            def _():
                rs_copy(u, way).wait_send()

            @pl.when(z != source[way])
            def _():
                ag_copy(u, way).wait_send()

        return carry

    lax.fori_loop(0, units, drain, 0)
    for k in range(1, n):
        disp_copy(k, me).wait_send()
        ret_copy(k, me).wait_send()
    for k in range(1, n):
        a, b = order[k]
        pltpu.make_async_remote_copy(
            src_ref=res.at[k],
            dst_ref=ret.at[partner(a, b, 1)],
            send_sem=ret_s.at[k],
            recv_sem=ret_r.at[k],
            device_id=(groups, me, z),
            device_id_type=MESH,
        ).wait_recv()

    rows = tokens.shape[0]
    label = lax.broadcasted_iota(jnp.int32, (rows, n * slot_rows), 1)
    chosen = [
        jnp.where(slots[:, k : k + 1] == label, 1.0, 0.0).astype(jnp.bfloat16)
        for k in range(slots.shape[1])
    ]
    tile = 2 * LANES if width % (2 * LANES) == 0 else LANES
    for c in range(width // tile):
        part = ret[:, :, c * tile : (c + 1) * tile].reshape(n * slot_rows, tile)
        mixed = jnp.zeros((rows, tile), jnp.float32)
        for k in range(slots.shape[1]):
            mixed = mixed + weights[:, k : k + 1] * jnp.dot(
                chosen[k], part, preferred_element_type=jnp.float32
            )
        out[:, c * tile : (c + 1) * tile] = mixed.astype(jnp.bfloat16)


def per_device(tokens, expert_ids, affinity, gate_up, down_proj):
    n = lax.axis_size("expert")
    depth = lax.axis_size("replica")
    rows, top = expert_ids.shape
    capacity = 5 * rows * top // (4 * n)
    slot_rows = -(-capacity // 16) * 16
    width = tokens.shape[1]
    hidden = down_proj.shape[1]
    slots = slot_table(expert_ids, n, slot_rows)
    weights = 2.5 * affinity / jnp.sum(affinity, axis=1, keepdims=True)
    order = [(0, 0)] + [(a, b) for a in range(1, n // 2) for b in range(2)] + [(0, 1)]
    units = n * SUBS
    sub = hidden // 2 // SUBS
    bf16 = jnp.bfloat16
    dma = pltpu.SemaphoreType.DMA
    vmem = pl.BlockSpec(memory_space=pltpu.VMEM)
    hbm = pl.BlockSpec(memory_space=pl.ANY)
    return pl.pallas_call(
        functools.partial(layer_kernel, n, depth, order),
        out_shape=jax.ShapeDtypeStruct((rows, width), bf16),
        in_specs=[vmem, vmem, vmem, vmem, hbm, hbm],
        out_specs=vmem,
        scratch_shapes=[
            pltpu.VMEM((2 * SUBS, 2 * width, sub), bf16),
            pltpu.VMEM((hidden, width), bf16),
            pltpu.VMEM((n - 1, slot_rows, width), bf16),
            pltpu.VMEM((n, slot_rows, width), bf16),
            pltpu.VMEM((n, 2 * slot_rows, 2 * width), bf16),
            pltpu.VMEM((2, 2 * slot_rows, sub), jnp.float32),
            pltpu.VMEM((units, 2, 2 * slot_rows, sub), bf16),
            pltpu.VMEM((units, 2, 2 * slot_rows, sub), bf16),
            pltpu.VMEM((units, 2, slot_rows, sub), bf16),
            pltpu.VMEM((n, slot_rows, width), bf16),
            pltpu.VMEM((n, slot_rows, width), bf16),
            dma((2 * SUBS, PIECES)),
            dma((1,)),
            dma((n,)),
            dma((n,)),
            dma((units, 2)),
            dma((units, 2)),
            dma((units, 2)),
            dma((units, 2)),
            dma((n,)),
            dma((n,)),
        ],
        compiler_params=pltpu.CompilerParams(
            collective_id=0, has_side_effects=True, vmem_limit_bytes=60 * 1024 * 1024
        ),
    )(tokens, slots.T, slots, weights, gate_up, down_proj)


def solution(mesh):
    placed = (
        P(("groups", "expert"), "replica"),
        P(("groups", "expert"), None),
        P(("groups", "expert"), None),
        P("expert", "replica", None, None),
        P("expert", None, "replica"),
    )
    return jax.shard_map(
        per_device,
        mesh=mesh,
        in_specs=placed,
        out_specs=P(("groups", "expert"), "replica"),
        check_vma=False,
    )
```

```python
import functools

import jax
import jax.numpy as jnp
from jax import lax
from jax.experimental import pallas as pl
from jax.experimental.pallas import tpu as pltpu
from jax.sharding import PartitionSpec as P

MESH = pl.DeviceIdType.MESH
LANES = 128
SUBS = 4
PIECES = 2
SKEW = 3


def layer_kernel(
    n, depth, order, tokens, ids_t, affinity_t, gate_up, down, out,
    w_buf, d_buf, outgoing, x_buf, xs, acc, rs_in, rs_out, hid, res, ret, chosen, share,
    w_sem, d_sem, disp_s, disp_r, rs_s, rs_r, ag_s, ag_r, ret_s, ret_r,
):
    groups = lax.axis_index("groups")
    me = lax.axis_index("expert")
    z = lax.axis_index("replica")
    chip, core = me // 2, me % 2
    slot_rows = x_buf.shape[1]
    width = x_buf.shape[2]
    hidden = d_buf.shape[0]
    half = hidden // 2
    sub = half // SUBS
    units = n * SUBS
    sink = (0, depth - 1)
    source = (depth - 1, 0)
    onward = (z - 1, z + 1)
    back = (z + 1, z - 1)

    cut = 2 * width // PIECES

    def w_copy(block, piece):
        return pltpu.make_async_copy(
            gate_up.at[0]
            .reshape(2 * width, hidden)
            .at[pl.ds(piece * cut, cut), pl.ds(pl.multiple_of(block * sub, sub), sub)],
            w_buf.at[block, pl.ds(piece * cut, cut)],
            w_sem.at[block, piece],
        )

    left = 1 - (2 * z) // depth
    for way in range(2):
        for s in range(SUBS):
            for piece in range(PIECES):
                w_copy(((way + left) % 2) * SUBS + s, piece).start()
    d_copy = pltpu.make_async_copy(down.at[0], d_buf, d_sem.at[0])
    d_copy.start()

    def partner(a, b, sign):
        return ((chip + sign * a + n // 2) % (n // 2)) * 2 + (core + b) % 2

    barrier = pltpu.get_barrier_semaphore()
    for a, b in order[1:]:
        pl.semaphore_signal(
            barrier, inc=1, device_id=(groups, partner(a, b, 1), z), device_id_type=MESH
        )

    @pl.when(z > 0)
    def _():
        pl.semaphore_signal(barrier, inc=1, device_id=(groups, me, z - 1), device_id_type=MESH)

    @pl.when(z < depth - 1)
    def _():
        pl.semaphore_signal(barrier, inc=1, device_id=(groups, me, z + 1), device_id_type=MESH)

    rows = tokens.shape[0]
    top = ids_t.shape[0]
    f32 = jnp.float32
    expert_label = lax.broadcasted_iota(jnp.int32, (-(-n // 16) * 16, rows), 0)
    named = [ids_t[k : k + 1, :] == expert_label for k in range(top)]
    per_row = sum(jnp.where(hit, 1.0, 0.0) for hit in named)
    first = lax.broadcasted_iota(jnp.int32, (rows, rows), 0)
    second = lax.broadcasted_iota(jnp.int32, (rows, rows), 1)
    earlier = jnp.where(first < second, 1.0, 0.0).astype(jnp.bfloat16)
    before = jnp.dot(per_row.astype(jnp.bfloat16), earlier, preferred_element_type=f32)
    slot = [
        ids_t[k : k + 1, :].astype(f32) * float(slot_rows)
        + jnp.sum(jnp.where(named[k], before, 0.0), axis=0, keepdims=True)
        for k in range(top)
    ]

    def pick(target):
        label = lax.broadcasted_iota(jnp.int32, (slot_rows, rows), 0)
        label = (label + target * slot_rows).astype(f32)
        total = sum(jnp.where(slot[k] == label, 1.0, 0.0) for k in range(top))
        return jnp.dot(
            total.astype(jnp.bfloat16), tokens[...], preferred_element_type=f32
        ).astype(jnp.bfloat16)

    x_buf[0] = pick(me)
    for k in range(1, n):
        a, b = order[k]
        outgoing[k - 1] = pick(partner(a, b, 1))

    at_end = jnp.logical_or(z == 0, z == depth - 1)

    @pl.when(at_end)
    def _():
        pl.semaphore_wait(barrier, n - 1 + min(1, depth - 1))

    @pl.when(jnp.logical_not(at_end))
    def _():
        pl.semaphore_wait(barrier, n + 1)

    def disp_copy(k, target):
        return pltpu.make_async_remote_copy(
            src_ref=outgoing.at[k - 1],
            dst_ref=x_buf.at[k],
            send_sem=disp_s.at[k],
            recv_sem=disp_r.at[k],
            device_id=(groups, target, z),
            device_id_type=MESH,
        )

    for k in range(1, n):
        a, b = order[k]
        disp_copy(k, partner(a, b, 1)).start()

    def column_of(line):
        return jnp.sum(jnp.where(first == second, line, 0.0), axis=1, keepdims=True)

    slot_label = lax.broadcasted_iota(jnp.int32, (rows, n * slot_rows), 1).astype(f32)
    whole = sum(affinity_t[k : k + 1, :] for k in range(top))
    for k in range(top):
        chosen[k] = jnp.where(column_of(slot[k]) == slot_label, 1.0, 0.0).astype(jnp.bfloat16)
        share[k] = jnp.broadcast_to(
            column_of(2.5 * affinity_t[k : k + 1, :] / whole), share.shape[1:]
        )

    def rs_copy(u, way):
        return pltpu.make_async_remote_copy(
            src_ref=rs_out.at[u, way],
            dst_ref=rs_in.at[u, way],
            send_sem=rs_s.at[u, way],
            recv_sem=rs_r.at[u, way],
            device_id=(groups, me, onward[way]),
            device_id_type=MESH,
        )

    def ag_copy(u, way):
        return pltpu.make_async_remote_copy(
            src_ref=hid.at[u, way],
            dst_ref=hid.at[u, way],
            send_sem=ag_s.at[u, way],
            recv_sem=ag_r.at[u, way],
            device_id=(groups, me, back[way]),
            device_id_type=MESH,
        )

    def ret_copy(k, target):
        return pltpu.make_async_remote_copy(
            src_ref=res.at[k],
            dst_ref=ret.at[me],
            send_sem=ret_s.at[k],
            recv_sem=ret_r.at[k],
            device_id=(groups, target, z),
            device_id_type=MESH,
        )

    row = lax.broadcasted_iota(jnp.int32, (LANES, 2 * LANES), 0)
    column = lax.broadcasted_iota(jnp.int32, (LANES, 2 * LANES), 1)
    spread = [
        jnp.where(column == 2 * row + j, 1.0, 0.0).astype(jnp.bfloat16) for j in range(2)
    ]

    position = (depth - 1 - z, z)
    nearest = jnp.minimum(position[0], position[1])
    furthest = jnp.maximum(position[0], position[1])
    fill = SKEW * (depth - 1)

    def live(u):
        return jnp.logical_and(u >= 0, u < units)

    def widen(k):
        @pl.when(k > 0)
        def _():
            disp_copy(k, me).wait_recv()

        for block in range(width // LANES):
            part = x_buf[k, :, block * LANES : (block + 1) * LANES]
            for j in range(2):
                xs[
                    k,
                    j * slot_rows : (j + 1) * slot_rows,
                    2 * block * LANES : 2 * (block + 1) * LANES,
                ] = jnp.dot(part, spread[j], preferred_element_type=jnp.float32).astype(
                    jnp.bfloat16
                )

    def multiply(u, way):
        block = way * SUBS + u % SUBS

        @pl.when(u < SUBS)
        def _():
            for piece in range(PIECES):
                w_copy(block, piece).wait()

        acc[way] = jnp.dot(
            xs[u // SUBS], w_buf[block], preferred_element_type=jnp.float32
        )

    def reduce_step(u, way):
        @pl.when(z != source[way])
        def _():
            rs_copy(u, way).wait_recv()
            acc[way] += rs_in[u, way].astype(jnp.float32)

        @pl.when(z != sink[way])
        def _():
            rs_out[u, way] = acc[way].astype(jnp.bfloat16)
            rs_copy(u, way).start()

        @pl.when(z == sink[way])
        def _():
            gate = acc[way, :slot_rows]
            hid[u, way] = (gate / (1.0 + jnp.exp(-gate)) * acc[way, slot_rows:]).astype(
                jnp.bfloat16
            )
            ag_copy(u, way).start()

    def gather_step(v, way):
        @pl.when(z != sink[way])
        def _():
            ag_copy(v, way).wait_recv()

            @pl.when(z != source[way])
            def _():
                ag_copy(v, way).start()

    def project(k):
        @pl.when(k == 0)
        def _():
            d_copy.wait()

        total = jnp.zeros((slot_rows, width), jnp.float32)
        for way in range(2):
            for i in range(SUBS):
                start = way * half + i * sub
                total = total + jnp.dot(
                    hid[k * SUBS + i, way],
                    d_buf[start : start + sub, :],
                    preferred_element_type=jnp.float32,
                )

        @pl.when(k == 0)
        def _():
            ret[me] = total.astype(jnp.bfloat16)

        for kk in range(1, n):
            a, b = order[kk]

            @pl.when(k == kk)
            def _():
                res[kk] = total.astype(jnp.bfloat16)
                ret_copy(kk, partner(a, b, -1)).start()

    def step(t, carry):
        lead = t - SKEW * nearest

        @pl.when(jnp.logical_and(live(lead), lead % SUBS == 0))
        def _():
            widen(lead // SUBS)

        for way in range(2):
            u = t - SKEW * position[way]

            @pl.when(live(u))
            def _():
                multiply(u, way)

        for way in range(2):
            u = t - SKEW * position[way]

            @pl.when(live(u))
            def _():
                reduce_step(u, way)

        for way in range(2):
            v = t - fill - SKEW * (depth - 1 - position[way])

            @pl.when(live(v))
            def _():
                gather_step(v, way)

        trail = t - fill - SKEW * furthest

        @pl.when(jnp.logical_and(live(trail), trail % SUBS == SUBS - 1))
        def _():
            project(trail // SUBS)

        return carry

    lax.fori_loop(0, units + 2 * fill, step, 0)

    def drain(u, carry):
        for way in range(2):

            @pl.when(z != sink[way])
            def _():
                rs_copy(u, way).wait_send()

            @pl.when(z != source[way])
            def _():
                ag_copy(u, way).wait_send()

        return carry

    lax.fori_loop(0, units, drain, 0)
    for k in range(1, n):
        disp_copy(k, me).wait_send()
        ret_copy(k, me).wait_send()
    for k in range(1, n):
        a, b = order[k]
        pltpu.make_async_remote_copy(
            src_ref=res.at[k],
            dst_ref=ret.at[partner(a, b, 1)],
            send_sem=ret_s.at[k],
            recv_sem=ret_r.at[k],
            device_id=(groups, me, z),
            device_id_type=MESH,
        ).wait_recv()

    tile = 2 * LANES if width % (2 * LANES) == 0 else LANES
    for c in range(width // tile):
        part = ret[:, :, c * tile : (c + 1) * tile].reshape(n * slot_rows, tile)
        mixed = jnp.zeros((rows, tile), jnp.float32)
        for k in range(top):
            mixed = mixed + share[k, :, :1] * jnp.dot(
                chosen[k], part, preferred_element_type=jnp.float32
            )
        out[:, c * tile : (c + 1) * tile] = mixed.astype(jnp.bfloat16)


def per_device(tokens, expert_ids, affinity, gate_up, down_proj):
    n = lax.axis_size("expert")
    depth = lax.axis_size("replica")
    rows, top = expert_ids.shape
    capacity = 5 * rows * top // (4 * n)
    slot_rows = -(-capacity // 16) * 16
    width = tokens.shape[1]
    hidden = down_proj.shape[1]
    order = [(0, 0)] + [(a, b) for a in range(1, n // 2) for b in range(2)] + [(0, 1)]
    units = n * SUBS
    sub = hidden // 2 // SUBS
    bf16 = jnp.bfloat16
    dma = pltpu.SemaphoreType.DMA
    vmem = pl.BlockSpec(memory_space=pltpu.VMEM)
    hbm = pl.BlockSpec(memory_space=pl.ANY)
    return pl.pallas_call(
        functools.partial(layer_kernel, n, depth, order),
        out_shape=jax.ShapeDtypeStruct((rows, width), bf16),
        in_specs=[vmem, vmem, vmem, hbm, hbm],
        out_specs=vmem,
        scratch_shapes=[
            pltpu.VMEM((2 * SUBS, 2 * width, sub), bf16),
            pltpu.VMEM((hidden, width), bf16),
            pltpu.VMEM((n - 1, slot_rows, width), bf16),
            pltpu.VMEM((n, slot_rows, width), bf16),
            pltpu.VMEM((n, 2 * slot_rows, 2 * width), bf16),
            pltpu.VMEM((2, 2 * slot_rows, sub), jnp.float32),
            pltpu.VMEM((units, 2, 2 * slot_rows, sub), bf16),
            pltpu.VMEM((units, 2, 2 * slot_rows, sub), bf16),
            pltpu.VMEM((units, 2, slot_rows, sub), bf16),
            pltpu.VMEM((n, slot_rows, width), bf16),
            pltpu.VMEM((n, slot_rows, width), bf16),
            pltpu.VMEM((top, rows, n * slot_rows), bf16),
            pltpu.VMEM((top, rows, LANES), jnp.float32),
            dma((2 * SUBS, PIECES)),
            dma((1,)),
            dma((n,)),
            dma((n,)),
            dma((units, 2)),
            dma((units, 2)),
            dma((units, 2)),
            dma((units, 2)),
            dma((n,)),
            dma((n,)),
        ],
        compiler_params=pltpu.CompilerParams(
            collective_id=0, has_side_effects=True, vmem_limit_bytes=60 * 1024 * 1024
        ),
    )(tokens, expert_ids.T, affinity.T, gate_up, down_proj)


def solution(mesh):
    placed = (
        P(("groups", "expert"), "replica"),
        P(("groups", "expert"), None),
        P(("groups", "expert"), None),
        P("expert", "replica", None, None),
        P("expert", None, "replica"),
    )
    return jax.shard_map(
        per_device,
        mesh=mesh,
        in_specs=placed,
        out_specs=P(("groups", "expert"), "replica"),
        check_vma=False,
    )
```

```python
import functools

import jax
import jax.numpy as jnp
from jax import lax
from jax.experimental import pallas as pl
from jax.experimental.pallas import tpu as pltpu
from jax.sharding import PartitionSpec as P

MESH = pl.DeviceIdType.MESH
LANES = 128
SUBS = 4
PIECES = 2
SKEW = 3


def layer_kernel(
    n, depth, order, tokens, ids_t, affinity_t, gate_up, down, out,
    w_buf, d_buf, outgoing, x_buf, xs, acc, rs_in, rs_out, hid, res, ret, chosen, share, total,
    w_sem, d_sem, disp_s, disp_r, rs_s, rs_r, ag_s, ag_r, ret_s, ret_r,
):
    groups = lax.axis_index("groups")
    me = lax.axis_index("expert")
    z = lax.axis_index("replica")
    chip, core = me // 2, me % 2
    slot_rows = x_buf.shape[1]
    width = x_buf.shape[2]
    hidden = d_buf.shape[0]
    half = hidden // 2
    sub = half // SUBS
    units = n * SUBS
    sink = (0, depth - 1)
    source = (depth - 1, 0)
    onward = (z - 1, z + 1)
    back = (z + 1, z - 1)

    cut = 2 * width // PIECES

    def w_copy(block, piece):
        return pltpu.make_async_copy(
            gate_up.at[0]
            .reshape(2 * width, hidden)
            .at[pl.ds(piece * cut, cut), pl.ds(pl.multiple_of(block * sub, sub), sub)],
            w_buf.at[block, pl.ds(piece * cut, cut)],
            w_sem.at[block, piece],
        )

    left = 1 - (2 * z) // depth
    for way in range(2):
        for s in range(SUBS):
            for piece in range(PIECES):
                w_copy(((way + left) % 2) * SUBS + s, piece).start()
    d_copy = pltpu.make_async_copy(down.at[0], d_buf, d_sem.at[0])
    d_copy.start()

    def partner(a, b, sign):
        return ((chip + sign * a + n // 2) % (n // 2)) * 2 + (core + b) % 2

    barrier = pltpu.get_barrier_semaphore()
    for a, b in order[1:]:
        pl.semaphore_signal(
            barrier, inc=1, device_id=(groups, partner(a, b, 1), z), device_id_type=MESH
        )

    @pl.when(z > 0)
    def _():
        pl.semaphore_signal(barrier, inc=1, device_id=(groups, me, z - 1), device_id_type=MESH)

    @pl.when(z < depth - 1)
    def _():
        pl.semaphore_signal(barrier, inc=1, device_id=(groups, me, z + 1), device_id_type=MESH)

    rows = tokens.shape[0]
    top = ids_t.shape[0]
    f32 = jnp.float32
    expert_label = lax.broadcasted_iota(jnp.int32, (-(-n // 16) * 16, rows), 0)
    named = [ids_t[k : k + 1, :] == expert_label for k in range(top)]
    per_row = sum(jnp.where(hit, 1.0, 0.0) for hit in named)
    first = lax.broadcasted_iota(jnp.int32, (rows, rows), 0)
    second = lax.broadcasted_iota(jnp.int32, (rows, rows), 1)
    earlier = jnp.where(first < second, 1.0, 0.0).astype(jnp.bfloat16)
    before = jnp.dot(per_row.astype(jnp.bfloat16), earlier, preferred_element_type=f32)
    slot = [
        ids_t[k : k + 1, :].astype(f32) * float(slot_rows)
        + jnp.sum(jnp.where(named[k], before, 0.0), axis=0, keepdims=True)
        for k in range(top)
    ]

    def pick(target):
        label = lax.broadcasted_iota(jnp.int32, (slot_rows, rows), 0)
        label = (label + target * slot_rows).astype(f32)
        hits = sum(jnp.where(slot[k] == label, 1.0, 0.0) for k in range(top))
        return jnp.dot(
            hits.astype(jnp.bfloat16), tokens[...], preferred_element_type=f32
        ).astype(jnp.bfloat16)

    x_buf[0] = pick(me)
    for k in range(1, n):
        a, b = order[k]
        outgoing[k - 1] = pick(partner(a, b, 1))

    at_end = jnp.logical_or(z == 0, z == depth - 1)

    @pl.when(at_end)
    def _():
        pl.semaphore_wait(barrier, n - 1 + min(1, depth - 1))

    @pl.when(jnp.logical_not(at_end))
    def _():
        pl.semaphore_wait(barrier, n + 1)

    def disp_copy(k, target):
        return pltpu.make_async_remote_copy(
            src_ref=outgoing.at[k - 1],
            dst_ref=x_buf.at[k],
            send_sem=disp_s.at[k],
            recv_sem=disp_r.at[k],
            device_id=(groups, target, z),
            device_id_type=MESH,
        )

    for k in range(1, n):
        a, b = order[k]
        disp_copy(k, partner(a, b, 1)).start()

    def column_of(line):
        return jnp.sum(jnp.where(first == second, line, 0.0), axis=1, keepdims=True)

    slot_label = lax.broadcasted_iota(jnp.int32, (rows, n * slot_rows), 1).astype(f32)
    whole = sum(affinity_t[k : k + 1, :] for k in range(top))
    for k in range(top):
        chosen[k] = jnp.where(column_of(slot[k]) == slot_label, 1.0, 0.0).astype(jnp.bfloat16)
        share[k] = jnp.broadcast_to(
            column_of(2.5 * affinity_t[k : k + 1, :] / whole), share.shape[1:]
        )

    def rs_copy(u, way):
        return pltpu.make_async_remote_copy(
            src_ref=rs_out.at[u, way],
            dst_ref=rs_in.at[u, way],
            send_sem=rs_s.at[u, way],
            recv_sem=rs_r.at[u, way],
            device_id=(groups, me, onward[way]),
            device_id_type=MESH,
        )

    def ag_copy(u, way):
        return pltpu.make_async_remote_copy(
            src_ref=hid.at[u, way],
            dst_ref=hid.at[u, way],
            send_sem=ag_s.at[u, way],
            recv_sem=ag_r.at[u, way],
            device_id=(groups, me, back[way]),
            device_id_type=MESH,
        )

    def ret_copy(k, target):
        return pltpu.make_async_remote_copy(
            src_ref=res.at[k],
            dst_ref=ret.at[me],
            send_sem=ret_s.at[k],
            recv_sem=ret_r.at[k],
            device_id=(groups, target, z),
            device_id_type=MESH,
        )

    row = lax.broadcasted_iota(jnp.int32, (LANES, 2 * LANES), 0)
    column = lax.broadcasted_iota(jnp.int32, (LANES, 2 * LANES), 1)
    spread = [
        jnp.where(column == 2 * row + j, 1.0, 0.0).astype(jnp.bfloat16) for j in range(2)
    ]

    position = (depth - 1 - z, z)
    nearest = jnp.minimum(position[0], position[1])
    furthest = jnp.maximum(position[0], position[1])
    fill = SKEW * (depth - 1)

    def live(u):
        return jnp.logical_and(u >= 0, u < units)

    def widen(k):
        @pl.when(k > 0)
        def _():
            disp_copy(k, me).wait_recv()

        for block in range(width // LANES):
            part = x_buf[k, :, block * LANES : (block + 1) * LANES]
            for j in range(2):
                xs[
                    k,
                    j * slot_rows : (j + 1) * slot_rows,
                    2 * block * LANES : 2 * (block + 1) * LANES,
                ] = jnp.dot(part, spread[j], preferred_element_type=jnp.float32).astype(
                    jnp.bfloat16
                )

    def multiply(u, way):
        block = way * SUBS + u % SUBS

        @pl.when(u < SUBS)
        def _():
            for piece in range(PIECES):
                w_copy(block, piece).wait()

        acc[way] = jnp.dot(
            xs[u // SUBS], w_buf[block], preferred_element_type=jnp.float32
        )

    def reduce_step(u, way):
        @pl.when(z != source[way])
        def _():
            rs_copy(u, way).wait_recv()
            acc[way] += rs_in[u, way].astype(jnp.float32)

        @pl.when(z != sink[way])
        def _():
            rs_out[u, way] = acc[way].astype(jnp.bfloat16)
            rs_copy(u, way).start()

        @pl.when(z == sink[way])
        def _():
            gate = acc[way, :slot_rows]
            hid[u, way] = (gate / (1.0 + jnp.exp(-gate)) * acc[way, slot_rows:]).astype(
                jnp.bfloat16
            )
            ag_copy(u, way).start()

    def gather_step(v, way):
        @pl.when(z != sink[way])
        def _():
            ag_copy(v, way).wait_recv()

            @pl.when(z != source[way])
            def _():
                ag_copy(v, way).start()

    def project(v, way):
        k, s = v // SUBS, v % SUBS
        start = pl.multiple_of((way * SUBS + s) * sub, sub)
        total[k] += jnp.dot(
            hid[v, way], d_buf[pl.ds(start, sub), :], preferred_element_type=f32
        )

    def send_back(k):
        @pl.when(k == 0)
        def _():
            ret[me] = total[0].astype(jnp.bfloat16)

        for kk in range(1, n):
            a, b = order[kk]

            @pl.when(k == kk)
            def _():
                res[kk] = total[kk].astype(jnp.bfloat16)
                ret_copy(kk, partner(a, b, -1)).start()

    def step(t, carry):
        lead = t - SKEW * nearest

        @pl.when(jnp.logical_and(live(lead), lead % SUBS == 0))
        def _():
            widen(lead // SUBS)

        for way in range(2):
            u = t - SKEW * position[way]

            @pl.when(live(u))
            def _():
                multiply(u, way)

        for way in range(2):
            u = t - SKEW * position[way]

            @pl.when(live(u))
            def _():
                reduce_step(u, way)

        for way in range(2):
            v = t - fill - SKEW * (depth - 1 - position[way])

            @pl.when(live(v))
            def _():
                gather_step(v, way)

        @pl.when(t == fill)
        def _():
            d_copy.wait()
            total[...] = jnp.zeros_like(total)

        for way in range(2):
            v = t - fill - SKEW * (depth - 1 - position[way])

            @pl.when(live(v))
            def _():
                project(v, way)

        trail = t - fill - SKEW * furthest

        @pl.when(jnp.logical_and(live(trail), trail % SUBS == SUBS - 1))
        def _():
            send_back(trail // SUBS)

        return carry

    lax.fori_loop(0, units + 2 * fill, step, 0)

    def drain(u, carry):
        for way in range(2):

            @pl.when(z != sink[way])
            def _():
                rs_copy(u, way).wait_send()

            @pl.when(z != source[way])
            def _():
                ag_copy(u, way).wait_send()

        return carry

    lax.fori_loop(0, units, drain, 0)
    for k in range(1, n):
        disp_copy(k, me).wait_send()
        ret_copy(k, me).wait_send()
    for k in range(1, n):
        a, b = order[k]
        pltpu.make_async_remote_copy(
            src_ref=res.at[k],
            dst_ref=ret.at[partner(a, b, 1)],
            send_sem=ret_s.at[k],
            recv_sem=ret_r.at[k],
            device_id=(groups, me, z),
            device_id_type=MESH,
        ).wait_recv()

    tile = 2 * LANES if width % (2 * LANES) == 0 else LANES
    for c in range(width // tile):
        part = ret[:, :, c * tile : (c + 1) * tile].reshape(n * slot_rows, tile)
        mixed = jnp.zeros((rows, tile), jnp.float32)
        for k in range(top):
            mixed = mixed + share[k, :, :1] * jnp.dot(
                chosen[k], part, preferred_element_type=jnp.float32
            )
        out[:, c * tile : (c + 1) * tile] = mixed.astype(jnp.bfloat16)


def per_device(tokens, expert_ids, affinity, gate_up, down_proj):
    n = lax.axis_size("expert")
    depth = lax.axis_size("replica")
    rows, top = expert_ids.shape
    capacity = 5 * rows * top // (4 * n)
    slot_rows = -(-capacity // 16) * 16
    width = tokens.shape[1]
    hidden = down_proj.shape[1]
    order = [(0, 0)] + [(a, b) for a in range(1, n // 2) for b in range(2)] + [(0, 1)]
    units = n * SUBS
    sub = hidden // 2 // SUBS
    bf16 = jnp.bfloat16
    dma = pltpu.SemaphoreType.DMA
    vmem = pl.BlockSpec(memory_space=pltpu.VMEM)
    hbm = pl.BlockSpec(memory_space=pl.ANY)
    return pl.pallas_call(
        functools.partial(layer_kernel, n, depth, order),
        out_shape=jax.ShapeDtypeStruct((rows, width), bf16),
        in_specs=[vmem, vmem, vmem, hbm, hbm],
        out_specs=vmem,
        scratch_shapes=[
            pltpu.VMEM((2 * SUBS, 2 * width, sub), bf16),
            pltpu.VMEM((hidden, width), bf16),
            pltpu.VMEM((n - 1, slot_rows, width), bf16),
            pltpu.VMEM((n, slot_rows, width), bf16),
            pltpu.VMEM((n, 2 * slot_rows, 2 * width), bf16),
            pltpu.VMEM((2, 2 * slot_rows, sub), jnp.float32),
            pltpu.VMEM((units, 2, 2 * slot_rows, sub), bf16),
            pltpu.VMEM((units, 2, 2 * slot_rows, sub), bf16),
            pltpu.VMEM((units, 2, slot_rows, sub), bf16),
            pltpu.VMEM((n, slot_rows, width), bf16),
            pltpu.VMEM((n, slot_rows, width), bf16),
            pltpu.VMEM((top, rows, n * slot_rows), bf16),
            pltpu.VMEM((top, rows, LANES), jnp.float32),
            pltpu.VMEM((n, slot_rows, width), jnp.float32),
            dma((2 * SUBS, PIECES)),
            dma((1,)),
            dma((n,)),
            dma((n,)),
            dma((units, 2)),
            dma((units, 2)),
            dma((units, 2)),
            dma((units, 2)),
            dma((n,)),
            dma((n,)),
        ],
        compiler_params=pltpu.CompilerParams(
            collective_id=0, has_side_effects=True, vmem_limit_bytes=60 * 1024 * 1024
        ),
    )(tokens, expert_ids.T, affinity.T, gate_up, down_proj)


def solution(mesh):
    placed = (
        P(("groups", "expert"), "replica"),
        P(("groups", "expert"), None),
        P(("groups", "expert"), None),
        P("expert", "replica", None, None),
        P("expert", None, "replica"),
    )
    return jax.shard_map(
        per_device,
        mesh=mesh,
        in_specs=placed,
        out_specs=P(("groups", "expert"), "replica"),
        check_vma=False,
    )
```

```python
import functools

import jax
import jax.numpy as jnp
from jax import lax
from jax.experimental import pallas as pl
from jax.experimental.pallas import tpu as pltpu
from jax.sharding import PartitionSpec as P

MESH = pl.DeviceIdType.MESH
LANES = 128
SUBS = 4
PIECES = 2
SKEW = 3


def layer_kernel(
    n, depth, order, tokens, ids_t, affinity_t, gate_up, down, out,
    w_buf, d_buf, outgoing, x_buf, xs, acc, rs_in, rs_out, hid, res, ret, chosen, share, total, stash,
    w_sem, d_sem, disp_s, disp_r, rs_s, rs_r, ag_s, ag_r, ret_s, ret_r,
):
    groups = lax.axis_index("groups")
    me = lax.axis_index("expert")
    z = lax.axis_index("replica")
    chip, core = me // 2, me % 2
    slot_rows = x_buf.shape[1]
    width = x_buf.shape[2]
    hidden = d_buf.shape[0]
    half = hidden // 2
    sub = half // SUBS
    units = n * SUBS
    sink = (0, depth - 1)
    source = (depth - 1, 0)
    onward = (z - 1, z + 1)
    back = (z + 1, z - 1)

    cut = 2 * width // PIECES

    def w_copy(block, piece):
        return pltpu.make_async_copy(
            gate_up.at[0]
            .reshape(2 * width, hidden)
            .at[pl.ds(piece * cut, cut), pl.ds(pl.multiple_of(block * sub, sub), sub)],
            w_buf.at[block, pl.ds(piece * cut, cut)],
            w_sem.at[block, piece],
        )

    left = 1 - (2 * z) // depth
    for way in range(2):
        for s in range(SUBS):
            for piece in range(PIECES):
                w_copy(((way + left) % 2) * SUBS + s, piece).start()
    d_copy = pltpu.make_async_copy(down.at[0], d_buf, d_sem.at[0])
    d_copy.start()

    def partner(a, b, sign):
        return ((chip + sign * a + n // 2) % (n // 2)) * 2 + (core + b) % 2

    barrier = pltpu.get_barrier_semaphore()
    for a, b in order[1:]:
        pl.semaphore_signal(
            barrier, inc=1, device_id=(groups, partner(a, b, 1), z), device_id_type=MESH
        )

    @pl.when(z > 0)
    def _():
        pl.semaphore_signal(barrier, inc=1, device_id=(groups, me, z - 1), device_id_type=MESH)

    @pl.when(z < depth - 1)
    def _():
        pl.semaphore_signal(barrier, inc=1, device_id=(groups, me, z + 1), device_id_type=MESH)

    rows = tokens.shape[0]
    top = ids_t.shape[0]
    f32 = jnp.float32
    expert_label = lax.broadcasted_iota(jnp.int32, (-(-n // 16) * 16, rows), 0)
    named = [ids_t[k : k + 1, :] == expert_label for k in range(top)]
    per_row = sum(jnp.where(hit, 1.0, 0.0) for hit in named)
    first = lax.broadcasted_iota(jnp.int32, (rows, rows), 0)
    second = lax.broadcasted_iota(jnp.int32, (rows, rows), 1)
    earlier = jnp.where(first < second, 1.0, 0.0).astype(jnp.bfloat16)
    before = jnp.dot(per_row.astype(jnp.bfloat16), earlier, preferred_element_type=f32)
    slot = [
        ids_t[k : k + 1, :].astype(f32) * float(slot_rows)
        + jnp.sum(jnp.where(named[k], before, 0.0), axis=0, keepdims=True)
        for k in range(top)
    ]

    def pick(target):
        label = lax.broadcasted_iota(jnp.int32, (slot_rows, rows), 0)
        label = (label + target * slot_rows).astype(f32)
        hits = sum(jnp.where(slot[k] == label, 1.0, 0.0) for k in range(top))
        return jnp.dot(
            hits.astype(jnp.bfloat16), tokens[...], preferred_element_type=f32
        ).astype(jnp.bfloat16)

    x_buf[0] = pick(me)
    for k in range(1, n):
        a, b = order[k]
        outgoing[k - 1] = pick(partner(a, b, 1))

    at_end = jnp.logical_or(z == 0, z == depth - 1)

    @pl.when(at_end)
    def _():
        pl.semaphore_wait(barrier, n - 1 + min(1, depth - 1))

    @pl.when(jnp.logical_not(at_end))
    def _():
        pl.semaphore_wait(barrier, n + 1)

    def disp_copy(k, target):
        return pltpu.make_async_remote_copy(
            src_ref=outgoing.at[k - 1],
            dst_ref=x_buf.at[k],
            send_sem=disp_s.at[k],
            recv_sem=disp_r.at[k],
            device_id=(groups, target, z),
            device_id_type=MESH,
        )

    for k in range(1, n):
        a, b = order[k]
        disp_copy(k, partner(a, b, 1)).start()

    def column_of(line):
        return jnp.sum(jnp.where(first == second, line, 0.0), axis=1, keepdims=True)

    slot_label = lax.broadcasted_iota(jnp.int32, (rows, n * slot_rows), 1).astype(f32)
    whole = sum(affinity_t[k : k + 1, :] for k in range(top))
    for k in range(top):
        chosen[k] = jnp.where(column_of(slot[k]) == slot_label, 1.0, 0.0).astype(jnp.bfloat16)
        share[k] = jnp.broadcast_to(
            column_of(2.5 * affinity_t[k : k + 1, :] / whole), share.shape[1:]
        )

    def rs_copy(u, way):
        return pltpu.make_async_remote_copy(
            src_ref=rs_out.at[u, way],
            dst_ref=rs_in.at[u, way],
            send_sem=rs_s.at[u, way],
            recv_sem=rs_r.at[u, way],
            device_id=(groups, me, onward[way]),
            device_id_type=MESH,
        )

    def ag_copy(u, way):
        return pltpu.make_async_remote_copy(
            src_ref=hid.at[u, way],
            dst_ref=hid.at[u, way],
            send_sem=ag_s.at[u, way],
            recv_sem=ag_r.at[u, way],
            device_id=(groups, me, back[way]),
            device_id_type=MESH,
        )

    def ret_copy(k, target):
        return pltpu.make_async_remote_copy(
            src_ref=res.at[k],
            dst_ref=ret.at[me],
            send_sem=ret_s.at[k],
            recv_sem=ret_r.at[k],
            device_id=(groups, target, z),
            device_id_type=MESH,
        )

    row = lax.broadcasted_iota(jnp.int32, (LANES, 2 * LANES), 0)
    column = lax.broadcasted_iota(jnp.int32, (LANES, 2 * LANES), 1)
    spread = [
        jnp.where(column == 2 * row + j, 1.0, 0.0).astype(jnp.bfloat16) for j in range(2)
    ]

    position = (depth - 1 - z, z)
    nearest = jnp.minimum(position[0], position[1])
    furthest = jnp.maximum(position[0], position[1])
    fill = SKEW * (depth - 1)

    def live(u):
        return jnp.logical_and(u >= 0, u < units)

    def widen(k):
        @pl.when(k > 0)
        def _():
            disp_copy(k, me).wait_recv()

        for block in range(width // LANES):
            part = x_buf[k, :, block * LANES : (block + 1) * LANES]
            for j in range(2):
                xs[
                    k,
                    j * slot_rows : (j + 1) * slot_rows,
                    2 * block * LANES : 2 * (block + 1) * LANES,
                ] = jnp.dot(part, spread[j], preferred_element_type=jnp.float32).astype(
                    jnp.bfloat16
                )

    def multiply(u, way):
        block = way * SUBS + u % SUBS

        @pl.when(u < SUBS)
        def _():
            for piece in range(PIECES):
                w_copy(block, piece).wait()

        k, s = u // SUBS, u % SUBS
        paired = k >= 2

        @pl.when(k < 2)
        def _():
            acc[way] = jnp.dot(xs[k], w_buf[block], preferred_element_type=f32)

        @pl.when(jnp.logical_and(paired, k % 2 == 0))
        def _():
            both = jnp.dot(
                xs[pl.ds(k, 2)].reshape(4 * slot_rows, 2 * width),
                w_buf[block],
                preferred_element_type=f32,
            )
            acc[way] = both[: 2 * slot_rows]
            stash[way, s] = both[2 * slot_rows :]

        @pl.when(jnp.logical_and(paired, k % 2 == 1))
        def _():
            acc[way] = stash[way, s]

    def reduce_step(u, way):
        @pl.when(z != source[way])
        def _():
            rs_copy(u, way).wait_recv()
            acc[way] += rs_in[u, way].astype(jnp.float32)

        @pl.when(z != sink[way])
        def _():
            rs_out[u, way] = acc[way].astype(jnp.bfloat16)
            rs_copy(u, way).start()

        @pl.when(z == sink[way])
        def _():
            gate = acc[way, :slot_rows]
            hid[u, way] = (gate / (1.0 + jnp.exp(-gate)) * acc[way, slot_rows:]).astype(
                jnp.bfloat16
            )
            ag_copy(u, way).start()

    def gather_step(v, way):
        @pl.when(z != sink[way])
        def _():
            ag_copy(v, way).wait_recv()

            @pl.when(z != source[way])
            def _():
                ag_copy(v, way).start()

    def project(v, way):
        k, s = v // SUBS, v % SUBS
        start = pl.multiple_of((way * SUBS + s) * sub, sub)
        total[k] += jnp.dot(
            hid[v, way], d_buf[pl.ds(start, sub), :], preferred_element_type=f32
        )

    def send_back(k):
        @pl.when(k == 0)
        def _():
            ret[me] = total[0].astype(jnp.bfloat16)

        for kk in range(1, n):
            a, b = order[kk]

            @pl.when(k == kk)
            def _():
                res[kk] = total[kk].astype(jnp.bfloat16)
                ret_copy(kk, partner(a, b, -1)).start()

    def step(t, carry):
        lead = t - SKEW * nearest

        @pl.when(jnp.logical_and(live(lead), lead % SUBS == 0))
        def _():
            k = lead // SUBS

            @pl.when(jnp.logical_or(k < 2, k % 2 == 0))
            def _():
                widen(k)

            @pl.when(jnp.logical_and(k >= 2, k % 2 == 0))
            def _():
                widen(k + 1)

        for way in range(2):
            u = t - SKEW * position[way]

            @pl.when(live(u))
            def _():
                multiply(u, way)

        for way in range(2):
            u = t - SKEW * position[way]

            @pl.when(live(u))
            def _():
                reduce_step(u, way)

        for way in range(2):
            v = t - fill - SKEW * (depth - 1 - position[way])

            @pl.when(live(v))
            def _():
                gather_step(v, way)

        @pl.when(t == fill)
        def _():
            d_copy.wait()
            total[...] = jnp.zeros_like(total)

        for way in range(2):
            v = t - fill - SKEW * (depth - 1 - position[way])

            @pl.when(live(v))
            def _():
                project(v, way)

        trail = t - fill - SKEW * furthest

        @pl.when(jnp.logical_and(live(trail), trail % SUBS == SUBS - 1))
        def _():
            send_back(trail // SUBS)

        return carry

    lax.fori_loop(0, units + 2 * fill, step, 0)

    def drain(u, carry):
        for way in range(2):

            @pl.when(z != sink[way])
            def _():
                rs_copy(u, way).wait_send()

            @pl.when(z != source[way])
            def _():
                ag_copy(u, way).wait_send()

        return carry

    lax.fori_loop(0, units, drain, 0)
    for k in range(1, n):
        disp_copy(k, me).wait_send()
        ret_copy(k, me).wait_send()
    for k in range(1, n):
        a, b = order[k]
        pltpu.make_async_remote_copy(
            src_ref=res.at[k],
            dst_ref=ret.at[partner(a, b, 1)],
            send_sem=ret_s.at[k],
            recv_sem=ret_r.at[k],
            device_id=(groups, me, z),
            device_id_type=MESH,
        ).wait_recv()

    tile = 2 * LANES if width % (2 * LANES) == 0 else LANES
    for c in range(width // tile):
        part = ret[:, :, c * tile : (c + 1) * tile].reshape(n * slot_rows, tile)
        mixed = jnp.zeros((rows, tile), jnp.float32)
        for k in range(top):
            mixed = mixed + share[k, :, :1] * jnp.dot(
                chosen[k], part, preferred_element_type=jnp.float32
            )
        out[:, c * tile : (c + 1) * tile] = mixed.astype(jnp.bfloat16)


def per_device(tokens, expert_ids, affinity, gate_up, down_proj):
    n = lax.axis_size("expert")
    depth = lax.axis_size("replica")
    rows, top = expert_ids.shape
    capacity = 5 * rows * top // (4 * n)
    slot_rows = -(-capacity // 16) * 16
    width = tokens.shape[1]
    hidden = down_proj.shape[1]
    order = [(0, 0)] + [(a, b) for a in range(1, n // 2) for b in range(2)] + [(0, 1)]
    units = n * SUBS
    sub = hidden // 2 // SUBS
    bf16 = jnp.bfloat16
    dma = pltpu.SemaphoreType.DMA
    vmem = pl.BlockSpec(memory_space=pltpu.VMEM)
    hbm = pl.BlockSpec(memory_space=pl.ANY)
    return pl.pallas_call(
        functools.partial(layer_kernel, n, depth, order),
        out_shape=jax.ShapeDtypeStruct((rows, width), bf16),
        in_specs=[vmem, vmem, vmem, hbm, hbm],
        out_specs=vmem,
        scratch_shapes=[
            pltpu.VMEM((2 * SUBS, 2 * width, sub), bf16),
            pltpu.VMEM((hidden, width), bf16),
            pltpu.VMEM((n - 1, slot_rows, width), bf16),
            pltpu.VMEM((n, slot_rows, width), bf16),
            pltpu.VMEM((n, 2 * slot_rows, 2 * width), bf16),
            pltpu.VMEM((2, 2 * slot_rows, sub), jnp.float32),
            pltpu.VMEM((units, 2, 2 * slot_rows, sub), bf16),
            pltpu.VMEM((units, 2, 2 * slot_rows, sub), bf16),
            pltpu.VMEM((units, 2, slot_rows, sub), bf16),
            pltpu.VMEM((n, slot_rows, width), bf16),
            pltpu.VMEM((n, slot_rows, width), bf16),
            pltpu.VMEM((top, rows, n * slot_rows), bf16),
            pltpu.VMEM((top, rows, LANES), jnp.float32),
            pltpu.VMEM((n, slot_rows, width), jnp.float32),
            pltpu.VMEM((2, SUBS, 2 * slot_rows, sub), jnp.float32),
            dma((2 * SUBS, PIECES)),
            dma((1,)),
            dma((n,)),
            dma((n,)),
            dma((units, 2)),
            dma((units, 2)),
            dma((units, 2)),
            dma((units, 2)),
            dma((n,)),
            dma((n,)),
        ],
        compiler_params=pltpu.CompilerParams(
            collective_id=0, has_side_effects=True, vmem_limit_bytes=60 * 1024 * 1024
        ),
    )(tokens, expert_ids.T, affinity.T, gate_up, down_proj)


def solution(mesh):
    placed = (
        P(("groups", "expert"), "replica"),
        P(("groups", "expert"), None),
        P(("groups", "expert"), None),
        P("expert", "replica", None, None),
        P("expert", None, "replica"),
    )
    return jax.shard_map(
        per_device,
        mesh=mesh,
        in_specs=placed,
        out_specs=P(("groups", "expert"), "replica"),
        check_vma=False,
    )
```

```python
import functools

import jax
import jax.numpy as jnp
from jax import lax
from jax.experimental import pallas as pl
from jax.experimental.pallas import tpu as pltpu
from jax.sharding import PartitionSpec as P

MESH = pl.DeviceIdType.MESH
LANES = 128
SUBS = 4
PIECES = 2
SKEW = 3


def layer_kernel(
    n, depth, order, tokens, ids_t, affinity_t, gate_up, down, out,
    w_buf, d_buf, outgoing, x_buf, xs, acc, rs_in, rs_out, hid, res, ret, chosen, share, total,
    w_sem, d_sem, disp_s, disp_r, rs_s, rs_r, ag_s, ag_r, ret_s, ret_r,
):
    groups = lax.axis_index("groups")
    me = lax.axis_index("expert")
    z = lax.axis_index("replica")
    chip, core = me // 2, me % 2
    slot_rows = x_buf.shape[1]
    width = x_buf.shape[2]
    hidden = d_buf.shape[0]
    half = hidden // 2
    sub = half // SUBS
    units = n * SUBS
    sink = (0, depth - 1)
    source = (depth - 1, 0)
    onward = (z - 1, z + 1)
    back = (z + 1, z - 1)

    cut = 2 * width // PIECES

    def w_copy(block, piece):
        return pltpu.make_async_copy(
            gate_up.at[0]
            .reshape(2 * width, hidden)
            .at[pl.ds(piece * cut, cut), pl.ds(pl.multiple_of(block * sub, sub), sub)],
            w_buf.at[block, pl.ds(piece * cut, cut)],
            w_sem.at[block, piece],
        )

    left = 1 - (2 * z) // depth
    for way in range(2):
        for s in range(SUBS):
            for piece in range(PIECES):
                w_copy(((way + left) % 2) * SUBS + s, piece).start()
    d_copy = pltpu.make_async_copy(down.at[0], d_buf, d_sem.at[0])
    d_copy.start()

    def partner(a, b, sign):
        return ((chip + sign * a + n // 2) % (n // 2)) * 2 + (core + b) % 2

    barrier = pltpu.get_barrier_semaphore()
    for a, b in order[1:]:
        pl.semaphore_signal(
            barrier, inc=1, device_id=(groups, partner(a, b, 1), z), device_id_type=MESH
        )

    @pl.when(z > 0)
    def _():
        pl.semaphore_signal(barrier, inc=1, device_id=(groups, me, z - 1), device_id_type=MESH)

    @pl.when(z < depth - 1)
    def _():
        pl.semaphore_signal(barrier, inc=1, device_id=(groups, me, z + 1), device_id_type=MESH)

    rows = tokens.shape[0]
    top = ids_t.shape[0]
    f32 = jnp.float32
    expert_label = lax.broadcasted_iota(jnp.int32, (-(-n // 16) * 16, rows), 0)
    named = [ids_t[k : k + 1, :] == expert_label for k in range(top)]
    per_row = sum(jnp.where(hit, 1.0, 0.0) for hit in named)
    first = lax.broadcasted_iota(jnp.int32, (rows, rows), 0)
    second = lax.broadcasted_iota(jnp.int32, (rows, rows), 1)
    earlier = jnp.where(first < second, 1.0, 0.0).astype(jnp.bfloat16)
    before = jnp.dot(per_row.astype(jnp.bfloat16), earlier, preferred_element_type=f32)
    slot = [
        ids_t[k : k + 1, :].astype(f32) * float(slot_rows)
        + jnp.sum(jnp.where(named[k], before, 0.0), axis=0, keepdims=True)
        for k in range(top)
    ]

    def pick(target):
        label = lax.broadcasted_iota(jnp.int32, (slot_rows, rows), 0)
        label = (label + target * slot_rows).astype(f32)
        hits = sum(jnp.where(slot[k] == label, 1.0, 0.0) for k in range(top))
        return jnp.dot(
            hits.astype(jnp.bfloat16), tokens[...], preferred_element_type=f32
        ).astype(jnp.bfloat16)

    x_buf[0] = pick(me)
    for k in range(1, n):
        a, b = order[k]
        outgoing[k - 1] = pick(partner(a, b, 1))

    at_end = jnp.logical_or(z == 0, z == depth - 1)

    @pl.when(at_end)
    def _():
        pl.semaphore_wait(barrier, n - 1 + min(1, depth - 1))

    @pl.when(jnp.logical_not(at_end))
    def _():
        pl.semaphore_wait(barrier, n + 1)

    def disp_copy(k, target):
        return pltpu.make_async_remote_copy(
            src_ref=outgoing.at[k - 1],
            dst_ref=x_buf.at[k],
            send_sem=disp_s.at[k],
            recv_sem=disp_r.at[k],
            device_id=(groups, target, z),
            device_id_type=MESH,
        )

    for k in range(1, n):
        a, b = order[k]
        disp_copy(k, partner(a, b, 1)).start()

    def column_of(line):
        return jnp.sum(jnp.where(first == second, line, 0.0), axis=1, keepdims=True)

    slot_label = lax.broadcasted_iota(jnp.int32, (rows, n * slot_rows), 1).astype(f32)
    whole = sum(affinity_t[k : k + 1, :] for k in range(top))
    def prepare_mix():
        for k in range(top):
            chosen[k] = jnp.where(column_of(slot[k]) == slot_label, 1.0, 0.0).astype(jnp.bfloat16)
            share[k] = jnp.broadcast_to(
                column_of(2.5 * affinity_t[k : k + 1, :] / whole), share.shape[1:]
            )

    def rs_copy(u, way):
        return pltpu.make_async_remote_copy(
            src_ref=rs_out.at[u, way],
            dst_ref=rs_in.at[u, way],
            send_sem=rs_s.at[u, way],
            recv_sem=rs_r.at[u, way],
            device_id=(groups, me, onward[way]),
            device_id_type=MESH,
        )

    def ag_copy(u, way):
        return pltpu.make_async_remote_copy(
            src_ref=hid.at[u, way],
            dst_ref=hid.at[u, way],
            send_sem=ag_s.at[u, way],
            recv_sem=ag_r.at[u, way],
            device_id=(groups, me, back[way]),
            device_id_type=MESH,
        )

    def ret_copy(k, target):
        return pltpu.make_async_remote_copy(
            src_ref=res.at[k],
            dst_ref=ret.at[me],
            send_sem=ret_s.at[k],
            recv_sem=ret_r.at[k],
            device_id=(groups, target, z),
            device_id_type=MESH,
        )

    row = lax.broadcasted_iota(jnp.int32, (LANES, 2 * LANES), 0)
    column = lax.broadcasted_iota(jnp.int32, (LANES, 2 * LANES), 1)
    spread = [
        jnp.where(column == 2 * row + j, 1.0, 0.0).astype(jnp.bfloat16) for j in range(2)
    ]

    position = (depth - 1 - z, z)
    nearest = jnp.minimum(position[0], position[1])
    furthest = jnp.maximum(position[0], position[1])
    fill = SKEW * (depth - 1)

    def live(u):
        return jnp.logical_and(u >= 0, u < units)

    def widen(k):
        @pl.when(k > 0)
        def _():
            disp_copy(k, me).wait_recv()

        for block in range(width // LANES):
            part = x_buf[k, :, block * LANES : (block + 1) * LANES]
            for j in range(2):
                xs[
                    k,
                    j * slot_rows : (j + 1) * slot_rows,
                    2 * block * LANES : 2 * (block + 1) * LANES,
                ] = jnp.dot(part, spread[j], preferred_element_type=jnp.float32).astype(
                    jnp.bfloat16
                )

    def multiply(u, way):
        block = way * SUBS + u % SUBS

        @pl.when(u < SUBS)
        def _():
            for piece in range(PIECES):
                w_copy(block, piece).wait()

        acc[way] = jnp.dot(
            xs[u // SUBS], w_buf[block], preferred_element_type=jnp.float32
        )

    def reduce_step(u, way):
        @pl.when(z != source[way])
        def _():
            rs_copy(u, way).wait_recv()
            acc[way] += rs_in[u, way].astype(jnp.float32)

        @pl.when(z != sink[way])
        def _():
            rs_out[u, way] = acc[way].astype(jnp.bfloat16)
            rs_copy(u, way).start()

        @pl.when(z == sink[way])
        def _():
            gate = acc[way, :slot_rows]
            hid[u, way] = (gate / (1.0 + jnp.exp(-gate)) * acc[way, slot_rows:]).astype(
                jnp.bfloat16
            )
            ag_copy(u, way).start()

    def gather_step(v, way):
        @pl.when(z != sink[way])
        def _():
            ag_copy(v, way).wait_recv()

            @pl.when(z != source[way])
            def _():
                ag_copy(v, way).start()

    def project(v, way):
        k, s = v // SUBS, v % SUBS
        start = pl.multiple_of((way * SUBS + s) * sub, sub)
        total[k] += jnp.dot(
            hid[v, way], d_buf[pl.ds(start, sub), :], preferred_element_type=f32
        )

    def send_back(k):
        @pl.when(k == 0)
        def _():
            ret[me] = total[0].astype(jnp.bfloat16)

        for kk in range(1, n):
            a, b = order[kk]

            @pl.when(k == kk)
            def _():
                res[kk] = total[kk].astype(jnp.bfloat16)
                ret_copy(kk, partner(a, b, -1)).start()

    def step(t, carry):
        lead = t - SKEW * nearest

        @pl.when(jnp.logical_and(live(lead), lead % SUBS == 0))
        def _():
            widen(lead // SUBS)

        for way in range(2):
            u = t - SKEW * position[way]

            @pl.when(live(u))
            def _():
                multiply(u, way)

        for way in range(2):
            u = t - SKEW * position[way]

            @pl.when(live(u))
            def _():
                reduce_step(u, way)

        for way in range(2):
            v = t - fill - SKEW * (depth - 1 - position[way])

            @pl.when(live(v))
            def _():
                gather_step(v, way)

        @pl.when(t == fill)
        def _():
            d_copy.wait()
            total[...] = jnp.zeros_like(total)
            prepare_mix()

        for way in range(2):
            v = t - fill - SKEW * (depth - 1 - position[way])

            @pl.when(live(v))
            def _():
                project(v, way)

        trail = t - fill - SKEW * furthest

        @pl.when(jnp.logical_and(live(trail), trail % SUBS == SUBS - 1))
        def _():
            send_back(trail // SUBS)

        return carry

    lax.fori_loop(0, units + 2 * fill, step, 0)

    def drain(u, carry):
        for way in range(2):

            @pl.when(z != sink[way])
            def _():
                rs_copy(u, way).wait_send()

            @pl.when(z != source[way])
            def _():
                ag_copy(u, way).wait_send()

        return carry

    lax.fori_loop(0, units, drain, 0)
    for k in range(1, n):
        disp_copy(k, me).wait_send()
        ret_copy(k, me).wait_send()
    for k in range(1, n):
        a, b = order[k]
        pltpu.make_async_remote_copy(
            src_ref=res.at[k],
            dst_ref=ret.at[partner(a, b, 1)],
            send_sem=ret_s.at[k],
            recv_sem=ret_r.at[k],
            device_id=(groups, me, z),
            device_id_type=MESH,
        ).wait_recv()

    tile = 2 * LANES if width % (2 * LANES) == 0 else LANES
    for c in range(width // tile):
        part = ret[:, :, c * tile : (c + 1) * tile].reshape(n * slot_rows, tile)
        mixed = jnp.zeros((rows, tile), jnp.float32)
        for k in range(top):
            mixed = mixed + share[k, :, :1] * jnp.dot(
                chosen[k], part, preferred_element_type=jnp.float32
            )
        out[:, c * tile : (c + 1) * tile] = mixed


def per_device(tokens, expert_ids, affinity, gate_up, down_proj):
    n = lax.axis_size("expert")
    depth = lax.axis_size("replica")
    rows, top = expert_ids.shape
    capacity = 5 * rows * top // (4 * n)
    slot_rows = -(-capacity // 16) * 16
    width = tokens.shape[1]
    hidden = down_proj.shape[1]
    order = [(0, 0)] + [(a, b) for a in range(1, n // 2) for b in range(2)] + [(0, 1)]
    units = n * SUBS
    sub = hidden // 2 // SUBS
    bf16 = jnp.bfloat16
    dma = pltpu.SemaphoreType.DMA
    vmem = pl.BlockSpec(memory_space=pltpu.VMEM)
    hbm = pl.BlockSpec(memory_space=pl.ANY)
    mixed = pl.pallas_call(
        functools.partial(layer_kernel, n, depth, order),
        out_shape=jax.ShapeDtypeStruct((rows, width), jnp.float32),
        in_specs=[vmem, vmem, vmem, hbm, hbm],
        out_specs=vmem,
        scratch_shapes=[
            pltpu.VMEM((2 * SUBS, 2 * width, sub), bf16),
            pltpu.VMEM((hidden, width), bf16),
            pltpu.VMEM((n - 1, slot_rows, width), bf16),
            pltpu.VMEM((n, slot_rows, width), bf16),
            pltpu.VMEM((n, 2 * slot_rows, 2 * width), bf16),
            pltpu.VMEM((2, 2 * slot_rows, sub), jnp.float32),
            pltpu.VMEM((units, 2, 2 * slot_rows, sub), bf16),
            pltpu.VMEM((units, 2, 2 * slot_rows, sub), bf16),
            pltpu.VMEM((units, 2, slot_rows, sub), bf16),
            pltpu.VMEM((n, slot_rows, width), bf16),
            pltpu.VMEM((n, slot_rows, width), bf16),
            pltpu.VMEM((top, rows, n * slot_rows), bf16),
            pltpu.VMEM((top, rows, LANES), jnp.float32),
            pltpu.VMEM((n, slot_rows, width), jnp.float32),
            dma((2 * SUBS, PIECES)),
            dma((1,)),
            dma((n,)),
            dma((n,)),
            dma((units, 2)),
            dma((units, 2)),
            dma((units, 2)),
            dma((units, 2)),
            dma((n,)),
            dma((n,)),
        ],
        compiler_params=pltpu.CompilerParams(
            collective_id=0, has_side_effects=True, vmem_limit_bytes=60 * 1024 * 1024
        ),
    )(tokens, expert_ids.T, affinity.T, gate_up, down_proj)
    return mixed.astype(bf16)


def solution(mesh):
    placed = (
        P(("groups", "expert"), "replica"),
        P(("groups", "expert"), None),
        P(("groups", "expert"), None),
        P("expert", "replica", None, None),
        P("expert", None, "replica"),
    )
    return jax.shard_map(
        per_device,
        mesh=mesh,
        in_specs=placed,
        out_specs=P(("groups", "expert"), "replica"),
        check_vma=False,
    )
```
